32 devices in a mesh: pulse: 4 (over z), range: 4 (over y, core), tile: 2 (over x).
Axes of the slice: x: 2, y: 2, z: 4, core: 2. Of those that a mesh axis runs over, the one named last changes fastest.
Arguments:
- echo: bfloat16 [2, 64, 32768], P(None, ('pulse', 'tile'), 'range'), may hold values from -6 to 6
- replica: bfloat16 [2, 4096], replicated, may hold values from -0.09375 to 0.09375
- interp: bfloat16 [32, 256, 128], P('range'), may hold values from -0.375 to 0.375
- band_start: int32 [64, 2, 4], P(('pulse', 'tile'), None, 'range'), may hold values from 0 to 7040, as said below
- visible: int32 [64, 2], P(('pulse', 'tile')), may hold values 0 or 1
- doppler: int32 [64], P(('pulse', 'tile')), may hold values from 0 to 511
- range_step: int32 [64], P(('pulse', 'tile')), may hold values from 0 to 4095
Outputs:
- image: float32 [2, 512, 4096], P(None, ('tile', 'pulse'), 'range')
The draws below stay inside these ranges and needn't reach their ends.
Inputs may be any that keep to these rules, and one draw needn't show every extreme that they name: band_start is counted within the 8192 bins of range block b and is a multiple of 128; the values 0 and 7040 both occur.
All inputs are finite; a program needn't handle non-finite values. No bound on the sum of `visible` on one device may be relied on, other than what follows from the above.
Results may differ from the reference program's by a relative error of at most 0.0047.
Values may be sent and summed in bfloat16 or wider, within the bound.
A program may use at most 64 MiB of HBM per device.

```python
import math
import jax
import jax.numpy as jnp
from jax import lax

CHIRP = 4096
SAMP_DEV = 8192
LINE_BLOCK = 128
RLINE_DEV = 1024
AZ_DEV = 64
TILES = 2
RBLOCKS = 4
NPULSE = 64
NR = 32768
BAND = 1152
NA = 512
NRG = 4096
N_PULSE = 4


def draw_band_start(key, part):
    largest_block = (SAMP_DEV - RLINE_DEV - LINE_BLOCK) // LINE_BLOCK
    values = jax.random.randint(key, (NPULSE, TILES, RBLOCKS), 0, largest_block + 1, dtype=jnp.int32) * LINE_BLOCK
    values = values.at[0, 0, 0].set(largest_block * LINE_BLOCK)
    return values.at[1, 0, 0].set(0)


def set_ends(result, key, least, high):
    place = [jax.random.randint(jax.random.fold_in(key, axis), (), 0, length) for axis, length in enumerate(result.shape)]
    main_axis = result.shape.index(max(result.shape))
    beside = place[:main_axis] + [(place[main_axis] + 1) % result.shape[main_axis]] + place[main_axis + 1:]
    return result.at[tuple(place)].set(least).at[tuple(beside)].set(high)


def level_of(rng, extent, shards, smallest, top_value):
    level = 1.0
    for dim, shards_of in shards:
        steps = jax.random.uniform(jax.random.fold_in(jax.random.fold_in(rng, 6), dim), (shards_of,), jnp.float32, smallest / len(shards), top_value / len(shards))
        level = level * jnp.repeat(jnp.exp(steps), extent[dim] // shards_of).reshape((-1,) + (1,) * (len(extent) - 1 - dim))
    return level


def scatter_about(stream_key, shape, deviation, limit, cuts=(), kind=jnp.bfloat16):
    array = deviation * jax.random.normal(stream_key, shape, jnp.float32)
    if cuts:
        array = array * level_of(stream_key, shape, cuts, -0.22, 0.18)
    return jnp.clip(array, -limit, limit).astype(kind)


def setup_inputs(seed: int = 0) -> dict:
    seeds = jax.random.split(jax.random.key(seed), 8)
    echo = scatter_about(seeds[0], (2, NPULSE, NR), 1.0, 6.0, ((1, 8), (2, 4)))
    replica = scatter_about(seeds[1], (2, CHIRP), CHIRP ** -0.5, 0.09375)
    interp = scatter_about(seeds[2], (NRG // LINE_BLOCK, 2 * LINE_BLOCK, LINE_BLOCK), (2 * LINE_BLOCK) ** -0.5, 0.375, ((0, 4),))
    band_start = draw_band_start(jax.random.fold_in(seeds[7], 71), 0)
    visible = set_ends((jax.random.randint(seeds[4], (NPULSE, TILES), 0, 4) < 3).astype(jnp.int32), jax.random.fold_in(seeds[4], 1), 0, 1)
    doppler = set_ends(jax.random.randint(seeds[5], (NPULSE,), 0, NA), jax.random.fold_in(seeds[5], 1), 0, NA - 1).astype(jnp.int32)
    range_step = set_ends(jax.random.randint(seeds[6], (NPULSE,), 0, NRG), jax.random.fold_in(seeds[6], 1), 0, NRG - 1).astype(jnp.int32)
    return {"echo": echo, "replica": replica, "interp": interp, "band_start": band_start, "visible": visible, "doppler": doppler, "range_step": range_step}


def toeplitz_block(padded, offset, block_width):
    segment = lax.dynamic_slice_in_dim(padded, offset, 2 * block_width + 1)
    repeated = jnp.tile(segment, block_width)[: 2 * block_width * block_width]
    skewed = repeated.reshape(block_width, 2 * block_width)
    return skewed[:, block_width:].T


def chirp_matrix(padded_real, padded_imag, offset, block_width):
    toep_real = toeplitz_block(padded_real, offset, block_width)
    toep_imag = toeplitz_block(padded_imag, offset, block_width)
    upper_rows = jnp.concatenate([toep_real, -toep_imag], axis=1)
    lower_rows = jnp.concatenate([toep_imag, toep_real], axis=1)
    return jnp.concatenate([upper_rows, lower_rows], axis=0)


def compress(extended, replica, block_width):
    chirp_len = replica.shape[1]
    pulses = extended.shape[1]
    total_blocks = extended.shape[2] // block_width
    out_blocks = total_blocks - chirp_len // block_width
    arranged = extended.reshape(2, pulses, total_blocks, block_width).transpose(1, 2, 0, 3)
    margin = jnp.zeros((2, block_width), replica.dtype)
    padded = jnp.concatenate([margin, replica, margin, margin[:, :1]], axis=1)

    def add_turn(turn_index, running):
        offset = (turn_index * block_width).astype(jnp.int32)
        matrix = chirp_matrix(padded[0], padded[1], offset, block_width)
        window = lax.dynamic_slice_in_dim(arranged, turn_index.astype(jnp.int32), out_blocks, 1)
        window = window.reshape(pulses * out_blocks, 2 * block_width)
        return running + jnp.dot(window, matrix, preferred_element_type=jnp.float32)

    start_total = jnp.zeros((pulses * out_blocks, 2 * block_width), jnp.float32)
    running = lax.fori_loop(0, chirp_len // block_width + 1, add_turn, start_total)
    shaped = running.reshape(pulses, out_blocks, 2, block_width).transpose(0, 2, 1, 3)
    return shaped.reshape(pulses, 2, out_blocks * block_width).astype(jnp.bfloat16)


def cut_bands(signals, first_bins, band_len):
    def cut_one(signal, first_bin):
        return lax.dynamic_slice_in_dim(signal, first_bin, band_len, 1)

    return jax.vmap(cut_one)(signals, first_bins)


def steer_lines(band_rows, interp_block, range_steps, first_line, range_total):
    pulses = band_rows.shape[0]
    block_count = interp_block.shape[0]
    line_block = interp_block.shape[2]
    pieces = band_rows.reshape(pulses, 2, block_count + 1, line_block)
    windows = jnp.concatenate([pieces[:, :, :-1], pieces[:, :, 1:]], axis=3)
    line_values = jnp.einsum("pcjb,jbl->pcjl", windows.astype(jnp.float32), interp_block.astype(jnp.float32))
    line_values = line_values.reshape(pulses, 2, block_count * line_block)
    line_number = first_line + jnp.arange(block_count * line_block, dtype=jnp.int32)
    phase_turns = (range_steps[:, None] * line_number[None, :]) % range_total
    phase_angle = phase_turns.astype(jnp.float32) * (2.0 * math.pi / range_total)
    cosine = jnp.cos(phase_angle)
    sine_part = jnp.sin(phase_angle)
    steered_real = line_values[:, 0] * cosine - line_values[:, 1] * sine_part
    steered_imag = line_values[:, 0] * sine_part + line_values[:, 1] * cosine
    return jnp.stack([steered_real, steered_imag], axis=1).astype(jnp.bfloat16)


def azimuth_factor(doppler_bins, visible_flags, line_number, azimuth_total, norm_scale):
    phase_turns = (line_number[:, None] * doppler_bins[None, :]) % azimuth_total
    phase_angle = phase_turns.astype(jnp.float32) * (2.0 * math.pi / azimuth_total)
    weight = visible_flags.astype(jnp.float32)[None, :] * norm_scale
    factor_real = (jnp.cos(phase_angle) * weight).astype(jnp.bfloat16)
    factor_imag = (jnp.sin(phase_angle) * weight).astype(jnp.bfloat16)
    return factor_real, factor_imag


def add_pulses(factor_real, factor_imag, steered):
    left_side = jnp.concatenate([factor_real, factor_imag], axis=1)
    steer_real = steered[:, 0]
    steer_imag = steered[:, 1]
    top_rows = jnp.concatenate([steer_real, steer_imag], axis=1)
    bottom_rows = jnp.concatenate([-steer_imag, steer_real], axis=1)
    right_side = jnp.concatenate([top_rows, bottom_rows], axis=0)
    return jnp.dot(left_side, right_side, preferred_element_type=jnp.float32)


def reference(echo, replica, interp, band_start, visible, doppler, range_step):
    half_chirp = CHIRP // 2
    block_width = min(256, half_chirp)
    extended = jnp.pad(echo, ((0, 0), (0, 0), (half_chirp, half_chirp)))
    compressed = compress(extended, replica, block_width)
    norm_scale = NPULSE ** -0.5
    range_pieces = RLINE_DEV // LINE_BLOCK
    strip_index = jnp.arange(N_PULSE * AZ_DEV, dtype=jnp.int32)

    def tile_image(tile_number):
        tile_flags = lax.dynamic_index_in_dim(visible, tile_number, 1, keepdims=False)
        line_number = tile_number * (N_PULSE * AZ_DEV) + strip_index
        factor_real, factor_imag = azimuth_factor(doppler, tile_flags, line_number, NA, norm_scale)
        columns = []
        for range_block in range(RBLOCKS):
            starts = lax.dynamic_index_in_dim(band_start[:, :, range_block], tile_number, 1, keepdims=False)
            band_rows = cut_bands(compressed, range_block * SAMP_DEV + starts, BAND)
            interp_block = interp[range_block * range_pieces:(range_block + 1) * range_pieces]
            steered = steer_lines(band_rows, interp_block, range_step, range_block * RLINE_DEV, NRG)
            summed = add_pulses(factor_real, factor_imag, steered)
            columns.append(summed.reshape(N_PULSE * AZ_DEV, 2, RLINE_DEV))
        return jnp.concatenate(columns, axis=2).transpose(1, 0, 2)

    tiles_out = lax.map(tile_image, jnp.arange(TILES, dtype=jnp.int32))
    return tiles_out.transpose(1, 0, 2, 3).reshape(2, NA, NRG)
```

```python
import functools
import math

import jax
import jax.numpy as jnp
from jax import lax
from jax.experimental import pallas as pl
from jax.experimental.pallas import tpu as pltpu
from jax.sharding import PartitionSpec as P

AZ_DEV = 64
LANES = 128
TILE_GROUP = 2
MESH = pl.DeviceIdType.MESH


def each(count, body):
    if count <= 16:
        for step in range(count):
            body(step)
    else:
        lax.fori_loop(0, count, lambda step, carry: (body(step), carry)[1], 0)


def wrap(value, total):
    if total & (total - 1) == 0:
        return value & (total - 1)
    return lax.rem(value, jnp.int32(total))


def image_kernel(
    sizes,
    starts_ref, visible_ref, doppler_ref, step_ref,
    echo_ref, replica_ref, interp_ref,
    out_ref,
    left_halo, right_halo, ext_re, ext_im, gat_re, gat_im, gat, chirp,
    turn_cos, turn_sin, own_bins, all_bins, own_rows, all_rows,
    halo_send, halo_recv, bins_send, bins_recv, rows_send, rows_recv,
):
    pulses, tiles, groups, ranges, band_blocks, chirp_blocks, samp_blocks, lines = sizes
    half_blocks = chirp_blocks // 2
    half = half_blocks * LANES
    samples = samp_blocks * LANES
    members = groups * tiles
    seen_blocks = band_blocks + chirp_blocks
    seen_pad = gat_re.shape[0] // (TILE_GROUP * pulses)
    group_id = lax.axis_index("pulse")
    tile_id = lax.axis_index("tile")
    range_id = lax.axis_index("range")
    me = group_id * tiles + tile_id

    def member(offset):
        other = lax.rem(me + offset, members)
        return other, {"pulse": other // tiles, "tile": lax.rem(other, tiles)}

    barrier = pltpu.get_barrier_semaphore()

    @pl.when(range_id > 0)
    def _():
        pl.semaphore_signal(barrier, inc=1, device_id={"range": range_id - 1}, device_id_type=MESH)

    @pl.when(range_id < ranges - 1)
    def _():
        pl.semaphore_signal(barrier, inc=1, device_id={"range": range_id + 1}, device_id_type=MESH)

    def greet(step):
        _, where = member(step + 1)
        pl.semaphore_signal(barrier, inc=1, device_id=where, device_id_type=MESH)

    each(members - 1, greet)
    neighbours = (range_id > 0).astype(jnp.int32) + (range_id < ranges - 1).astype(jnp.int32)
    pl.semaphore_wait(barrier, members - 1 + neighbours)

    to_left = pltpu.make_async_remote_copy(
        src_ref=echo_ref.at[:, pl.ds(0, half)], dst_ref=right_halo,
        send_sem=halo_send.at[0], recv_sem=halo_recv.at[0],
        device_id={"range": lax.max(range_id - 1, 0)}, device_id_type=MESH,
    )
    to_right = pltpu.make_async_remote_copy(
        src_ref=echo_ref.at[:, pl.ds(samples - half, half)], dst_ref=left_halo,
        send_sem=halo_send.at[1], recv_sem=halo_recv.at[1],
        device_id={"range": lax.min(range_id + 1, ranges - 1)}, device_id_type=MESH,
    )

    @pl.when(range_id > 0)
    def _():
        to_left.start()

    @pl.when(range_id < ranges - 1)
    def _():
        to_right.start()

    lane = lax.broadcasted_iota(jnp.int32, (8, LANES), 1)
    row = lax.broadcasted_iota(jnp.int32, (8, LANES), 0)
    lane_pulse = lane % pulses
    bins = jnp.zeros((8, LANES), jnp.int32)
    for q in range(pulses):
        bins = jnp.where(lane_pulse == q, doppler_ref[q], bins)

    def fill_bins(tile):
        flags = jnp.zeros((8, LANES), jnp.int32)
        for q in range(pulses):
            flags = jnp.where(lane_pulse == q, visible_ref[q, tile], flags)
        own_bins[tile] = jnp.where(row == 0, bins, flags)

    each(tiles, fill_bins)

    def bins_copy(step):
        other, where = member(step + 1)
        return pltpu.make_async_remote_copy(
            src_ref=own_bins.at[lax.rem(other, tiles)], dst_ref=all_bins.at[me],
            send_sem=bins_send.at[step], recv_sem=bins_recv.at[step],
            device_id=where, device_id_type=MESH,
        )

    each(members - 1, lambda step: bins_copy(step).start())
    all_bins[me] = own_bins[tile_id]

    wide = (chirp_blocks + 1) * LANES

    def shifted(part):
        taps = replica_ref[...].astype(jnp.float32)[part:part + 1, :]
        taps = jnp.concatenate([taps, jnp.zeros((1, LANES), jnp.float32)], axis=1)
        spread = jnp.broadcast_to(taps, (LANES, wide))
        return pltpu.roll(spread, 0, 1, stride=1, stride_axis=0).astype(jnp.bfloat16)

    shifted_re = shifted(0)
    for turn in range(chirp_blocks + 1):
        block = shifted_re[:, turn * LANES:(turn + 1) * LANES]
        chirp[turn, :LANES, :LANES] = block
        chirp[turn, LANES:, LANES:] = block
    shifted_im = shifted(1)
    for turn in range(chirp_blocks + 1):
        block = shifted_im[:, turn * LANES:(turn + 1) * LANES]
        chirp[turn, :LANES, LANES:] = block
        chirp[turn, LANES:, :LANES] = -block

    line_number = range_id * lines + lax.broadcasted_iota(jnp.int32, (pulses, lines), 1)
    pulse_row = lax.broadcasted_iota(jnp.int32, (pulses, lines), 0)
    steps = jnp.zeros((pulses, lines), jnp.int32)
    for q in range(pulses):
        steps = jnp.where(pulse_row == q, step_ref[q], steps)
    range_total = lines * ranges
    angle = wrap(steps * line_number, range_total).astype(jnp.float32) * (2.0 * math.pi / range_total)
    turn_cos[...] = jnp.cos(angle)
    turn_sin[...] = jnp.sin(angle)

    def lay(block, values):
        ext_re[block * pulses:(block + 1) * pulses, :] = values[:pulses]
        ext_im[block * pulses:(block + 1) * pulses, :] = values[pulses:]

    for block in range(samp_blocks):
        lay(half_blocks + block, echo_ref[:, block * LANES:(block + 1) * LANES].astype(jnp.float32))
    filled = samp_blocks + 2 * half_blocks
    tail = ext_re.shape[0] - filled * pulses
    ext_re[filled * pulses:, :] = jnp.zeros((tail, LANES), jnp.float32)
    ext_im[filled * pulses:, :] = jnp.zeros((tail, LANES), jnp.float32)

    @pl.when(range_id > 0)
    def _():
        to_right.wait_recv()

    @pl.when(range_id == 0)
    def _():
        left_halo[...] = jnp.zeros_like(left_halo)

    @pl.when(range_id < ranges - 1)
    def _():
        to_left.wait_recv()

    @pl.when(range_id == ranges - 1)
    def _():
        right_halo[...] = jnp.zeros_like(right_halo)

    for block in range(half_blocks):
        lay(block, left_halo[:, block * LANES:(block + 1) * LANES].astype(jnp.float32))
        lay(
            half_blocks + samp_blocks + block,
            right_halo[:, block * LANES:(block + 1) * LANES].astype(jnp.float32),
        )

    rows = TILE_GROUP * pulses

    def tile_pair(pair):
        for which in range(TILE_GROUP):
            for q in range(pulses):
                first = starts_ref[q, pair * TILE_GROUP + which] // LANES
                source = pl.ds(first * pulses + q, seen_pad, stride=pulses)
                target = pl.ds(which * pulses + q, seen_pad, stride=rows)
                gat_re[target, :] = ext_re[source, :]
                gat_im[target, :] = ext_im[source, :]
        gat[:, :LANES] = gat_re[...].astype(jnp.bfloat16)
        gat[:, LANES:] = gat_im[...].astype(jnp.bfloat16)
        total = jnp.zeros((band_blocks * rows, 2 * LANES), jnp.float32)
        for turn in range(chirp_blocks + 1):
            total = total + lax.dot_general(
                gat[turn * rows:(turn + band_blocks) * rows, :], chirp[turn],
                (((1,), (1,)), ((), ())), preferred_element_type=jnp.float32,
            )
        bands = total.astype(jnp.bfloat16)
        for j in range(band_blocks - 1):
            here = bands[j * rows:(j + 1) * rows]
            after = bands[(j + 1) * rows:(j + 2) * rows]
            window = jnp.concatenate(
                [
                    jnp.concatenate([here[:, :LANES], after[:, :LANES]], axis=1),
                    jnp.concatenate([here[:, LANES:], after[:, LANES:]], axis=1),
                ],
                axis=0,
            )
            values = jnp.dot(window, interp_ref[j], preferred_element_type=jnp.float32)
            cosine = turn_cos[:, j * LANES:(j + 1) * LANES]
            sine = turn_sin[:, j * LANES:(j + 1) * LANES]
            for which in range(TILE_GROUP):
                real = values[which * pulses:(which + 1) * pulses]
                imag = values[rows + which * pulses:rows + (which + 1) * pulses]
                steered = jnp.concatenate(
                    [real * cosine - imag * sine, real * sine + imag * cosine], axis=0
                )
                own_rows[pair * TILE_GROUP + which, :, j * LANES:(j + 1) * LANES] = steered.astype(jnp.bfloat16)

    each(tiles // TILE_GROUP, tile_pair)

    def rows_copy(step):
        other, where = member(step + 1)
        return pltpu.make_async_remote_copy(
            src_ref=own_rows.at[lax.rem(other, tiles)], dst_ref=all_rows.at[me],
            send_sem=rows_send.at[step], recv_sem=rows_recv.at[step],
            device_id=where, device_id_type=MESH,
        )

    each(members - 1, lambda step: rows_copy(step).start())
    all_rows[me] = own_rows[tile_id]

    each(members - 1, lambda step: bins_copy(step).wait_recv())
    azimuth_total = AZ_DEV * members
    norm_scale = (pulses * members) ** (-0.5)
    per_member = 2 * pulses
    per_chunk = LANES // per_member
    first_line = tile_id * (groups * AZ_DEV) + group_id * AZ_DEV
    az_line = first_line + lax.broadcasted_iota(jnp.int32, (AZ_DEV, LANES), 0)
    az_lane = lax.broadcasted_iota(jnp.int32, (AZ_DEV, LANES), 1)
    is_imag = (az_lane // pulses) % 2 == 1
    factors = []
    for chunk in range(members // per_chunk):
        known = jnp.zeros((8, LANES), jnp.int32)
        for at in range(per_chunk):
            known = jnp.where(lane // per_member == at, all_bins[chunk * per_chunk + at], known)
        angle = wrap(az_line * known[0:1, :], azimuth_total).astype(jnp.float32) * (2.0 * math.pi / azimuth_total)
        weight = known[1:2, :].astype(jnp.float32) * norm_scale
        factor_re = jnp.cos(angle) * weight
        factor_im = jnp.sin(angle) * weight
        factors.append(
            jnp.concatenate(
                [jnp.where(is_imag, -factor_im, factor_re), jnp.where(is_imag, factor_re, factor_im)], axis=0
            ).astype(jnp.bfloat16)
        )

    each(members - 1, lambda step: rows_copy(step).wait_recv())
    for chunk in range(members // per_chunk):
        right = all_rows[chunk * per_chunk:(chunk + 1) * per_chunk].reshape(LANES, lines)
        part = jnp.dot(factors[chunk], right, preferred_element_type=jnp.float32)
        if chunk == 0:
            out_ref[...] = part
        else:
            out_ref[...] += part

    @pl.when(range_id > 0)
    def _():
        to_left.wait_send()

    @pl.when(range_id < ranges - 1)
    def _():
        to_right.wait_send()

    each(members - 1, lambda step: bins_copy(step).wait_send())
    each(members - 1, lambda step: rows_copy(step).wait_send())


def local(echo, replica, interp, band_start, visible, doppler, range_step):
    chirp_blocks = replica.shape[1] // LANES
    pulses = echo.shape[1]
    samples = echo.shape[2]
    samp_blocks = samples // LANES
    lines = interp.shape[0] * interp.shape[2]
    band_blocks = interp.shape[0] + 1
    tiles = lax.axis_size("tile")
    groups = lax.axis_size("pulse")
    ranges = lax.axis_size("range")
    members = tiles * groups
    half = chirp_blocks * LANES // 2
    rows = TILE_GROUP * pulses
    seen_pad = -(-(band_blocks + chirp_blocks) // 8) * 8
    ext_blocks = samp_blocks + chirp_blocks + 8
    sizes = (pulses, tiles, groups, ranges, band_blocks, chirp_blocks, samp_blocks, lines)
    smem = pl.BlockSpec(memory_space=pltpu.SMEM)
    vmem = pl.BlockSpec(memory_space=pltpu.VMEM)
    image = pl.pallas_call(
        functools.partial(image_kernel, sizes),
        out_shape=jax.ShapeDtypeStruct((2 * AZ_DEV, lines), jnp.float32),
        in_specs=[smem] * 4 + [vmem] * 3,
        out_specs=vmem,
        scratch_shapes=[
            pltpu.VMEM((2 * pulses, half), jnp.bfloat16),
            pltpu.VMEM((2 * pulses, half), jnp.bfloat16),
            pltpu.VMEM((ext_blocks * pulses, LANES), jnp.float32),
            pltpu.VMEM((ext_blocks * pulses, LANES), jnp.float32),
            pltpu.VMEM((seen_pad * rows, LANES), jnp.float32),
            pltpu.VMEM((seen_pad * rows, LANES), jnp.float32),
            pltpu.VMEM((seen_pad * rows, 2 * LANES), jnp.bfloat16),
            pltpu.VMEM((chirp_blocks + 1, 2 * LANES, 2 * LANES), jnp.bfloat16),
            pltpu.VMEM((pulses, lines), jnp.float32),
            pltpu.VMEM((pulses, lines), jnp.float32),
            pltpu.VMEM((tiles, 8, LANES), jnp.int32),
            pltpu.VMEM((members, 8, LANES), jnp.int32),
            pltpu.VMEM((tiles, 2 * pulses, lines), jnp.bfloat16),
            pltpu.VMEM((members, 2 * pulses, lines), jnp.bfloat16),
            pltpu.SemaphoreType.DMA((2,)),
            pltpu.SemaphoreType.DMA((2,)),
            pltpu.SemaphoreType.DMA((members - 1,)),
            pltpu.SemaphoreType.DMA((members - 1,)),
            pltpu.SemaphoreType.DMA((members - 1,)),
            pltpu.SemaphoreType.DMA((members - 1,)),
        ],
        compiler_params=pltpu.CompilerParams(
            collective_id=0, has_side_effects=True, vmem_limit_bytes=40 * 1024 * 1024
        ),
        name="backproject",
    )(
        band_start.reshape(pulses, tiles), visible, doppler, range_step,
        echo.reshape(2 * pulses, samples), replica, interp,
    )
    return image.reshape(2, AZ_DEV, lines)


def solution(mesh):
    in_specs = (
        P(None, ("pulse", "tile"), "range"),
        P(),
        P("range", None, None),
        P(("pulse", "tile"), None, "range"),
        P(("pulse", "tile"), None),
        P(("pulse", "tile")),
        P(("pulse", "tile")),
    )
    out_specs = P(None, ("tile", "pulse"), "range")
    return jax.shard_map(local, mesh=mesh, in_specs=in_specs, out_specs=out_specs, check_vma=False)
```

```python
import functools
import math

import jax
import jax.numpy as jnp
from jax import lax
from jax.experimental import pallas as pl
from jax.experimental.pallas import tpu as pltpu
from jax.sharding import PartitionSpec as P

AZ_DEV = 64
LANES = 128
TILE_GROUP = 2
MESH = pl.DeviceIdType.MESH


def each(count, body):
    if count <= 16:
        for step in range(count):
            body(step)
    else:
        lax.fori_loop(0, count, lambda step, carry: (body(step), carry)[1], 0)


def wrap(value, total):
    if total & (total - 1) == 0:
        return value & (total - 1)
    return lax.rem(value, jnp.int32(total))


def image_kernel(
    sizes,
    starts_in, visible_in, doppler_in, step_in,
    echo_in, replica_in, interp_in,
    all_rows, factor_ref,
    starts_ref, visible_ref, doppler_ref, step_ref,
    echo_ref, replica_ref, interp_ref, load_sem,
    left_halo, right_halo, ext_re, ext_im, gat_re, gat_im, gat, chirp,
    turn_cos, turn_sin, own_bins, all_bins, own_rows, own_sem,
    halo_send, halo_recv, bins_send, bins_recv, rows_send, rows_recv,
):
    pulses, tiles, groups, ranges, band_blocks, chirp_blocks, samp_blocks, lines = sizes
    half_blocks = chirp_blocks // 2
    half = half_blocks * LANES
    samples = samp_blocks * LANES
    members = groups * tiles
    seen_blocks = band_blocks + chirp_blocks
    seen_pad = gat_re.shape[0] // (TILE_GROUP * pulses)
    group_id = lax.axis_index("pulse")
    tile_id = lax.axis_index("tile")
    range_id = lax.axis_index("range")
    me = group_id * tiles + tile_id

    def member(offset):
        other = lax.rem(me + offset, members)
        return other, {"pulse": other // tiles, "tile": lax.rem(other, tiles)}

    places = (
        (step_in, step_ref), (doppler_in, doppler_ref), (visible_in, visible_ref), (starts_in, starts_ref),
        (replica_in, replica_ref), (echo_in, echo_ref), (interp_in, interp_ref),
    )
    loads = [
        pltpu.make_async_copy(there, here, load_sem.at[place]) for place, (there, here) in enumerate(places)
    ]
    load_step, load_doppler, load_visible, load_starts, load_replica, load_echo, load_interp = loads
    for load in loads:
        load.start()

    barrier = pltpu.get_barrier_semaphore()

    @pl.when(range_id > 0)
    def _():
        pl.semaphore_signal(barrier, inc=1, device_id={"range": range_id - 1}, device_id_type=MESH)

    @pl.when(range_id < ranges - 1)
    def _():
        pl.semaphore_signal(barrier, inc=1, device_id={"range": range_id + 1}, device_id_type=MESH)

    def greet(step):
        _, where = member(step + 1)
        pl.semaphore_signal(barrier, inc=1, device_id=where, device_id_type=MESH)

    each(members - 1, greet)
    load_step.wait()
    line_number = range_id * lines + lax.broadcasted_iota(jnp.int32, (pulses, lines), 1)
    pulse_row = lax.broadcasted_iota(jnp.int32, (pulses, lines), 0)
    steps = jnp.zeros((pulses, lines), jnp.int32)
    for q in range(pulses):
        steps = jnp.where(pulse_row == q, step_ref[q], steps)
    range_total = lines * ranges
    angle = wrap(steps * line_number, range_total).astype(jnp.float32) * (2.0 * math.pi / range_total)
    turn_cos[...] = jnp.cos(angle)
    turn_sin[...] = jnp.sin(angle)

    neighbours = (range_id > 0).astype(jnp.int32) + (range_id < ranges - 1).astype(jnp.int32)
    pl.semaphore_wait(barrier, members - 1 + neighbours)

    to_left = pltpu.make_async_remote_copy(
        src_ref=echo_in.at[:, pl.ds(0, half)], dst_ref=right_halo,
        send_sem=halo_send.at[0], recv_sem=halo_recv.at[0],
        device_id={"range": lax.max(range_id - 1, 0)}, device_id_type=MESH,
    )
    to_right = pltpu.make_async_remote_copy(
        src_ref=echo_in.at[:, pl.ds(samples - half, half)], dst_ref=left_halo,
        send_sem=halo_send.at[1], recv_sem=halo_recv.at[1],
        device_id={"range": lax.min(range_id + 1, ranges - 1)}, device_id_type=MESH,
    )

    @pl.when(range_id > 0)
    def _():
        to_left.start()

    @pl.when(range_id < ranges - 1)
    def _():
        to_right.start()

    load_doppler.wait()
    load_visible.wait()
    load_starts.wait()
    lane = lax.broadcasted_iota(jnp.int32, (8, LANES), 1)
    row = lax.broadcasted_iota(jnp.int32, (8, LANES), 0)
    lane_pulse = lane % pulses
    bins = jnp.zeros((8, LANES), jnp.int32)
    for q in range(pulses):
        bins = jnp.where(lane_pulse == q, doppler_ref[q], bins)

    def fill_bins(tile):
        flags = jnp.zeros((8, LANES), jnp.int32)
        for q in range(pulses):
            flags = jnp.where(lane_pulse == q, visible_ref[tile, q], flags)
        own_bins[tile] = jnp.where(row == 0, bins, flags)

    each(tiles, fill_bins)

    def bins_copy(step):
        other, where = member(step + 1)
        return pltpu.make_async_remote_copy(
            src_ref=own_bins.at[lax.rem(other, tiles)], dst_ref=all_bins.at[me],
            send_sem=bins_send.at[step], recv_sem=bins_recv.at[step],
            device_id=where, device_id_type=MESH,
        )

    each(members - 1, lambda step: bins_copy(step).start())
    all_bins[me] = own_bins[tile_id]

    load_replica.wait()

    wide = (chirp_blocks + 1) * LANES

    def shifted(part):
        taps = replica_ref[...].astype(jnp.float32)[part:part + 1, :]
        taps = jnp.concatenate([taps, jnp.zeros((1, LANES), jnp.float32)], axis=1)
        spread = jnp.broadcast_to(taps, (LANES, wide))
        return pltpu.roll(spread, 0, 1, stride=1, stride_axis=0).astype(jnp.bfloat16)

    shifted_re = shifted(0)
    for turn in range(chirp_blocks + 1):
        block = shifted_re[:, turn * LANES:(turn + 1) * LANES]
        chirp[turn, :LANES, :LANES] = block
        chirp[turn, LANES:, LANES:] = block
    shifted_im = shifted(1)
    for turn in range(chirp_blocks + 1):
        block = shifted_im[:, turn * LANES:(turn + 1) * LANES]
        chirp[turn, :LANES, LANES:] = block
        chirp[turn, LANES:, :LANES] = -block

    def lay(block, values):
        ext_re[block * pulses:(block + 1) * pulses, :] = values[:pulses]
        ext_im[block * pulses:(block + 1) * pulses, :] = values[pulses:]

    load_echo.wait()
    for block in range(samp_blocks):
        lay(half_blocks + block, echo_ref[:, block * LANES:(block + 1) * LANES].astype(jnp.float32))
    filled = samp_blocks + 2 * half_blocks
    tail = ext_re.shape[0] - filled * pulses
    ext_re[filled * pulses:, :] = jnp.zeros((tail, LANES), jnp.float32)
    ext_im[filled * pulses:, :] = jnp.zeros((tail, LANES), jnp.float32)

    @pl.when(range_id > 0)
    def _():
        to_right.wait_recv()

    @pl.when(range_id == 0)
    def _():
        left_halo[...] = jnp.zeros_like(left_halo)

    @pl.when(range_id < ranges - 1)
    def _():
        to_left.wait_recv()

    @pl.when(range_id == ranges - 1)
    def _():
        right_halo[...] = jnp.zeros_like(right_halo)

    for block in range(half_blocks):
        lay(block, left_halo[:, block * LANES:(block + 1) * LANES].astype(jnp.float32))
        lay(
            half_blocks + samp_blocks + block,
            right_halo[:, block * LANES:(block + 1) * LANES].astype(jnp.float32),
        )

    load_interp.wait()

    rows = TILE_GROUP * pulses

    def tile_pair(pair):
        for which in range(TILE_GROUP):
            for q in range(pulses):
                first = starts_ref[pair * TILE_GROUP + which, 0, q] // LANES
                source = pl.ds(first * pulses + q, seen_pad, stride=pulses)
                target = pl.ds(which * pulses + q, seen_pad, stride=rows)
                gat_re[target, :] = ext_re[source, :]
                gat_im[target, :] = ext_im[source, :]
        gat[:, :LANES] = gat_re[...].astype(jnp.bfloat16)
        gat[:, LANES:] = gat_im[...].astype(jnp.bfloat16)
        total = jnp.zeros((band_blocks * rows, 2 * LANES), jnp.float32)
        for turn in range(chirp_blocks + 1):
            total = total + lax.dot_general(
                gat[turn * rows:(turn + band_blocks) * rows, :], chirp[turn],
                (((1,), (1,)), ((), ())), preferred_element_type=jnp.float32,
            )
        bands = total.astype(jnp.bfloat16)
        for j in range(band_blocks - 1):
            here = bands[j * rows:(j + 1) * rows]
            after = bands[(j + 1) * rows:(j + 2) * rows]
            window = jnp.concatenate(
                [
                    jnp.concatenate([here[:, :LANES], after[:, :LANES]], axis=1),
                    jnp.concatenate([here[:, LANES:], after[:, LANES:]], axis=1),
                ],
                axis=0,
            )
            values = jnp.dot(window, interp_ref[j], preferred_element_type=jnp.float32)
            cosine = turn_cos[:, j * LANES:(j + 1) * LANES]
            sine = turn_sin[:, j * LANES:(j + 1) * LANES]
            for which in range(TILE_GROUP):
                real = values[which * pulses:(which + 1) * pulses]
                imag = values[rows + which * pulses:rows + (which + 1) * pulses]
                steered = jnp.concatenate(
                    [real * cosine - imag * sine, real * sine + imag * cosine], axis=0
                )
                own_rows[pair * TILE_GROUP + which, :, j * LANES:(j + 1) * LANES] = steered.astype(jnp.bfloat16)

    each(tiles // TILE_GROUP, tile_pair)

    def rows_copy(step):
        other, where = member(step + 1)
        return pltpu.make_async_remote_copy(
            src_ref=own_rows.at[lax.rem(other, tiles)], dst_ref=all_rows.at[me],
            send_sem=rows_send.at[step], recv_sem=rows_recv.at[step],
            device_id=where, device_id_type=MESH,
        )

    each(members - 1, lambda step: rows_copy(step).start())
    keep_own = pltpu.make_async_copy(own_rows.at[tile_id], all_rows.at[me], own_sem)
    keep_own.start()

    each(members - 1, lambda step: bins_copy(step).wait_recv())
    azimuth_total = AZ_DEV * members
    norm_scale = (pulses * members) ** (-0.5)
    per_member = 2 * pulses
    per_chunk = LANES // per_member
    first_line = tile_id * (groups * AZ_DEV) + group_id * AZ_DEV
    az_line = first_line + lax.broadcasted_iota(jnp.int32, (AZ_DEV, LANES), 0)
    az_lane = lax.broadcasted_iota(jnp.int32, (AZ_DEV, LANES), 1)
    is_imag = (az_lane // pulses) % 2 == 1
    for chunk in range(members // per_chunk):
        known = jnp.zeros((8, LANES), jnp.int32)
        for at in range(per_chunk):
            known = jnp.where(lane // per_member == at, all_bins[chunk * per_chunk + at], known)
        angle = wrap(az_line * known[0:1, :], azimuth_total).astype(jnp.float32) * (2.0 * math.pi / azimuth_total)
        weight = known[1:2, :].astype(jnp.float32) * norm_scale
        factor_re = jnp.cos(angle) * weight
        factor_im = jnp.sin(angle) * weight
        factor_ref[:, chunk * LANES:(chunk + 1) * LANES] = jnp.concatenate(
            [jnp.where(is_imag, -factor_im, factor_re), jnp.where(is_imag, factor_re, factor_im)], axis=0
        ).astype(jnp.bfloat16)

    each(members - 1, lambda step: rows_copy(step).wait_recv())
    keep_own.wait()

    @pl.when(range_id > 0)
    def _():
        to_left.wait_send()

    @pl.when(range_id < ranges - 1)
    def _():
        to_right.wait_send()

    each(members - 1, lambda step: bins_copy(step).wait_send())
    each(members - 1, lambda step: rows_copy(step).wait_send())


def local(echo, replica, interp, band_start, visible, doppler, range_step):
    chirp_blocks = replica.shape[1] // LANES
    pulses = echo.shape[1]
    samples = echo.shape[2]
    samp_blocks = samples // LANES
    lines = interp.shape[0] * interp.shape[2]
    band_blocks = interp.shape[0] + 1
    tiles = lax.axis_size("tile")
    groups = lax.axis_size("pulse")
    ranges = lax.axis_size("range")
    members = tiles * groups
    half = chirp_blocks * LANES // 2
    rows = TILE_GROUP * pulses
    seen_pad = -(-(band_blocks + chirp_blocks) // 8) * 8
    ext_blocks = samp_blocks + chirp_blocks + 8
    sizes = (pulses, tiles, groups, ranges, band_blocks, chirp_blocks, samp_blocks, lines)
    hbm = pl.BlockSpec(memory_space=pl.ANY)
    vmem = pl.BlockSpec(memory_space=pltpu.VMEM)
    rows_out, factors = pl.pallas_call(
        functools.partial(image_kernel, sizes),
        out_shape=(
            jax.ShapeDtypeStruct((members, 2 * pulses, lines), jnp.bfloat16),
            jax.ShapeDtypeStruct((2 * AZ_DEV, members * 2 * pulses), jnp.bfloat16),
        ),
        in_specs=[hbm] * 7,
        out_specs=(hbm, vmem),
        scratch_shapes=[
            pltpu.SMEM((tiles, 1, pulses), jnp.int32),
            pltpu.SMEM((tiles, pulses), jnp.int32),
            pltpu.SMEM((pulses,), jnp.int32),
            pltpu.SMEM((pulses,), jnp.int32),
            pltpu.VMEM((2 * pulses, samples), jnp.bfloat16),
            pltpu.VMEM(replica.shape, jnp.bfloat16),
            pltpu.VMEM(interp.shape, jnp.bfloat16),
            pltpu.SemaphoreType.DMA((7,)),
            pltpu.VMEM((2 * pulses, half), jnp.bfloat16),
            pltpu.VMEM((2 * pulses, half), jnp.bfloat16),
            pltpu.VMEM((ext_blocks * pulses, LANES), jnp.float32),
            pltpu.VMEM((ext_blocks * pulses, LANES), jnp.float32),
            pltpu.VMEM((seen_pad * rows, LANES), jnp.float32),
            pltpu.VMEM((seen_pad * rows, LANES), jnp.float32),
            pltpu.VMEM((seen_pad * rows, 2 * LANES), jnp.bfloat16),
            pltpu.VMEM((chirp_blocks + 1, 2 * LANES, 2 * LANES), jnp.bfloat16),
            pltpu.VMEM((pulses, lines), jnp.float32),
            pltpu.VMEM((pulses, lines), jnp.float32),
            pltpu.VMEM((tiles, 8, LANES), jnp.int32),
            pltpu.VMEM((members, 8, LANES), jnp.int32),
            pltpu.VMEM((tiles, 2 * pulses, lines), jnp.bfloat16),
            pltpu.SemaphoreType.DMA,
            pltpu.SemaphoreType.DMA((2,)),
            pltpu.SemaphoreType.DMA((2,)),
            pltpu.SemaphoreType.DMA((members - 1,)),
            pltpu.SemaphoreType.DMA((members - 1,)),
            pltpu.SemaphoreType.DMA((members - 1,)),
            pltpu.SemaphoreType.DMA((members - 1,)),
        ],
        compiler_params=pltpu.CompilerParams(
            collective_id=0, has_side_effects=True, vmem_limit_bytes=60 * 1024 * 1024
        ),
        name="backproject",
    )(
        band_start.transpose(1, 2, 0), visible.T, doppler, range_step,
        echo.reshape(2 * pulses, samples), replica, interp,
    )
    image = jnp.dot(
        factors, rows_out.reshape(members * 2 * pulses, lines), preferred_element_type=jnp.float32
    )
    return image.reshape(2, AZ_DEV, lines)


def solution(mesh):
    in_specs = (
        P(None, ("pulse", "tile"), "range"),
        P(),
        P("range", None, None),
        P(("pulse", "tile"), None, "range"),
        P(("pulse", "tile"), None),
        P(("pulse", "tile")),
        P(("pulse", "tile")),
    )
    out_specs = P(None, ("tile", "pulse"), "range")
    return jax.shard_map(local, mesh=mesh, in_specs=in_specs, out_specs=out_specs, check_vma=False)
```

```python
import functools
import math

import jax
import jax.numpy as jnp
from jax import lax
from jax.experimental import pallas as pl
from jax.experimental.pallas import tpu as pltpu
from jax.sharding import PartitionSpec as P

AZ_DEV = 64
LANES = 128
TILE_GROUP = 2
MESH = pl.DeviceIdType.MESH


def each(count, body, first=0):
    if count <= 16:
        for step in range(first, count):
            body(step)
    else:
        lax.fori_loop(first, count, lambda step, carry: (body(step), carry)[1], 0)


def wrap(value, total):
    if total & (total - 1) == 0:
        return value & (total - 1)
    return lax.rem(value, jnp.int32(total))


def image_kernel(
    sizes,
    starts_in, visible_in, doppler_in, step_in,
    echo_in, replica_in, interp_in,
    all_rows, factor_ref,
    starts_ref, visible_ref, doppler_ref, step_ref,
    echo_ref, replica_ref, interp_ref, load_sem,
    left_halo, right_halo, ext_re, ext_im, gat_re, gat_im, gat, chirp,
    turn_cos, turn_sin, own_bins, all_bins, own_rows, own_sem,
    halo_send, halo_recv, bins_send, bins_recv, rows_send, rows_recv, relay_send,
):
    pulses, tiles, groups, ranges, band_blocks, chirp_blocks, samp_blocks, lines = sizes
    half_blocks = chirp_blocks // 2
    half = half_blocks * LANES
    samples = samp_blocks * LANES
    members = groups * tiles
    seen_blocks = band_blocks + chirp_blocks
    seen_pad = gat_re.shape[0] // (TILE_GROUP * pulses)
    group_id = lax.axis_index("pulse")
    tile_id = lax.axis_index("tile")
    range_id = lax.axis_index("range")
    me = group_id * tiles + tile_id

    turns = [2 % groups] + [turn for turn in range(1, groups) if turn != 2 % groups] + [0]

    def others(body, which=None):
        for turn in turns if which is None else which:
            each(tiles, functools.partial(body, turn), first=1 if turn == 0 else 0)

    def member(turn, step):
        group = lax.rem(group_id + turn, groups)
        tile = lax.rem(tile_id + step, tiles)
        return tile, {"pulse": group, "tile": tile}

    places = (
        (step_in, step_ref), (doppler_in, doppler_ref), (visible_in, visible_ref), (starts_in, starts_ref),
        (replica_in, replica_ref), (echo_in, echo_ref), (interp_in, interp_ref),
    )
    loads = [
        pltpu.make_async_copy(there, here, load_sem.at[place]) for place, (there, here) in enumerate(places)
    ]
    load_step, load_doppler, load_visible, load_starts, load_replica, load_echo, load_interp = loads
    for load in loads:
        load.start()

    barrier = pltpu.get_barrier_semaphore()

    @pl.when(range_id > 0)
    def _():
        pl.semaphore_signal(barrier, inc=1, device_id={"range": range_id - 1}, device_id_type=MESH)

    @pl.when(range_id < ranges - 1)
    def _():
        pl.semaphore_signal(barrier, inc=1, device_id={"range": range_id + 1}, device_id_type=MESH)

    def greet(turn, step):
        _, where = member(turn, step)
        pl.semaphore_signal(barrier, inc=1, device_id=where, device_id_type=MESH)

    others(greet)
    load_step.wait()
    line_number = range_id * lines + lax.broadcasted_iota(jnp.int32, (pulses, lines), 1)
    pulse_row = lax.broadcasted_iota(jnp.int32, (pulses, lines), 0)
    steps = jnp.zeros((pulses, lines), jnp.int32)
    for q in range(pulses):
        steps = jnp.where(pulse_row == q, step_ref[q], steps)
    range_total = lines * ranges
    angle = wrap(steps * line_number, range_total).astype(jnp.float32) * (2.0 * math.pi / range_total)
    turn_cos[...] = jnp.cos(angle)
    turn_sin[...] = jnp.sin(angle)

    neighbours = (range_id > 0).astype(jnp.int32) + (range_id < ranges - 1).astype(jnp.int32)
    pl.semaphore_wait(barrier, members - 1 + neighbours)

    to_left = pltpu.make_async_remote_copy(
        src_ref=echo_in.at[:, pl.ds(0, half)], dst_ref=right_halo,
        send_sem=halo_send.at[0], recv_sem=halo_recv.at[0],
        device_id={"range": lax.max(range_id - 1, 0)}, device_id_type=MESH,
    )
    to_right = pltpu.make_async_remote_copy(
        src_ref=echo_in.at[:, pl.ds(samples - half, half)], dst_ref=left_halo,
        send_sem=halo_send.at[1], recv_sem=halo_recv.at[1],
        device_id={"range": lax.min(range_id + 1, ranges - 1)}, device_id_type=MESH,
    )

    @pl.when(range_id > 0)
    def _():
        to_left.start()

    @pl.when(range_id < ranges - 1)
    def _():
        to_right.start()

    load_doppler.wait()
    load_visible.wait()
    load_starts.wait()
    lane = lax.broadcasted_iota(jnp.int32, (8, LANES), 1)
    row = lax.broadcasted_iota(jnp.int32, (8, LANES), 0)
    lane_pulse = lane % pulses
    bins = jnp.zeros((8, LANES), jnp.int32)
    for q in range(pulses):
        bins = jnp.where(lane_pulse == q, doppler_ref[q], bins)

    def fill_bins(tile):
        flags = jnp.zeros((8, LANES), jnp.int32)
        for q in range(pulses):
            flags = jnp.where(lane_pulse == q, visible_ref[tile, q], flags)
        own_bins[tile] = jnp.where(row == 0, bins, flags)

    each(tiles, fill_bins)

    def bins_copy(turn, step):
        tile, where = member(turn, step)
        return pltpu.make_async_remote_copy(
            src_ref=own_bins.at[tile], dst_ref=all_bins.at[me],
            send_sem=bins_send.at[turn * tiles + step], recv_sem=bins_recv.at[turn * tiles + step],
            device_id=where, device_id_type=MESH,
        )

    others(lambda turn, step: bins_copy(turn, step).start())
    all_bins[me] = own_bins[tile_id]

    load_replica.wait()

    wide = (chirp_blocks + 1) * LANES

    def shifted(part):
        taps = replica_ref[...].astype(jnp.float32)[part:part + 1, :]
        taps = jnp.concatenate([taps, jnp.zeros((1, LANES), jnp.float32)], axis=1)
        spread = jnp.broadcast_to(taps, (LANES, wide))
        return pltpu.roll(spread, 0, 1, stride=1, stride_axis=0).astype(jnp.bfloat16)

    shifted_re = shifted(0)
    for turn in range(chirp_blocks + 1):
        block = shifted_re[:, turn * LANES:(turn + 1) * LANES]
        chirp[turn, :LANES, :LANES] = block
        chirp[turn, LANES:, LANES:] = block
    shifted_im = shifted(1)
    for turn in range(chirp_blocks + 1):
        block = shifted_im[:, turn * LANES:(turn + 1) * LANES]
        chirp[turn, :LANES, LANES:] = block
        chirp[turn, LANES:, :LANES] = -block

    def lay(block, values):
        ext_re[block * pulses:(block + 1) * pulses, :] = values[:pulses]
        ext_im[block * pulses:(block + 1) * pulses, :] = values[pulses:]

    load_echo.wait()
    for block in range(samp_blocks):
        lay(half_blocks + block, echo_ref[:, block * LANES:(block + 1) * LANES].astype(jnp.float32))
    filled = samp_blocks + 2 * half_blocks
    tail = ext_re.shape[0] - filled * pulses
    ext_re[filled * pulses:, :] = jnp.zeros((tail, LANES), jnp.float32)
    ext_im[filled * pulses:, :] = jnp.zeros((tail, LANES), jnp.float32)

    @pl.when(range_id > 0)
    def _():
        to_right.wait_recv()

    @pl.when(range_id == 0)
    def _():
        left_halo[...] = jnp.zeros_like(left_halo)

    @pl.when(range_id < ranges - 1)
    def _():
        to_left.wait_recv()

    @pl.when(range_id == ranges - 1)
    def _():
        right_halo[...] = jnp.zeros_like(right_halo)

    for block in range(half_blocks):
        lay(block, left_halo[:, block * LANES:(block + 1) * LANES].astype(jnp.float32))
        lay(
            half_blocks + samp_blocks + block,
            right_halo[:, block * LANES:(block + 1) * LANES].astype(jnp.float32),
        )

    load_interp.wait()

    rows = TILE_GROUP * pulses
    cut = band_blocks // 2 + 1
    parts = [(0, cut), (cut, band_blocks)] if tiles == TILE_GROUP else [(0, band_blocks)]
    spans = [
        pl.ds(max(start - 1, 0) * LANES, (stop - 1 - max(start - 1, 0)) * LANES) for start, stop in parts
    ]

    def gather(pair):
        for which in range(TILE_GROUP):
            for q in range(pulses):
                first = starts_ref[pair * TILE_GROUP + which, 0, q] // LANES
                source = pl.ds(first * pulses + q, seen_pad, stride=pulses)
                target = pl.ds(which * pulses + q, seen_pad, stride=rows)
                gat_re[target, :] = ext_re[source, :]
                gat_im[target, :] = ext_im[source, :]
        gat[:, :LANES] = gat_re[...].astype(jnp.bfloat16)
        gat[:, LANES:] = gat_im[...].astype(jnp.bfloat16)

    def steer(pair, start, stop, before):
        total = jnp.zeros(((stop - start) * rows, 2 * LANES), jnp.float32)
        for turn in range(chirp_blocks + 1):
            total = total + lax.dot_general(
                gat[(turn + start) * rows:(turn + stop) * rows, :], chirp[turn],
                (((1,), (1,)), ((), ())), preferred_element_type=jnp.float32,
            )
        made = total.astype(jnp.bfloat16)
        bands = before + [made[j * rows:(j + 1) * rows] for j in range(stop - start)]
        for here, after, j in zip(bands, bands[1:], range(start - len(before), stop - 1)):
            window = jnp.concatenate(
                [
                    jnp.concatenate([here[:, :LANES], after[:, :LANES]], axis=1),
                    jnp.concatenate([here[:, LANES:], after[:, LANES:]], axis=1),
                ],
                axis=0,
            )
            values = jnp.dot(window, interp_ref[j], preferred_element_type=jnp.float32)
            cosine = turn_cos[:, j * LANES:(j + 1) * LANES]
            sine = turn_sin[:, j * LANES:(j + 1) * LANES]
            for which in range(TILE_GROUP):
                real = values[which * pulses:(which + 1) * pulses]
                imag = values[rows + which * pulses:rows + (which + 1) * pulses]
                steered = jnp.concatenate(
                    [real * cosine - imag * sine, real * sine + imag * cosine], axis=0
                )
                own_rows[pair * TILE_GROUP + which, :, j * LANES:(j + 1) * LANES] = steered.astype(jnp.bfloat16)
        return bands[-1:]

    relay = groups == 4
    relays = jnp.logical_or(group_id == 1, group_id == groups - 2)

    def rows_copy(part, turn, step):
        tile, where = member(turn, step)
        return pltpu.make_async_remote_copy(
            src_ref=own_rows.at[tile, :, spans[part]], dst_ref=all_rows.at[me, :, spans[part]],
            send_sem=rows_send.at[part, turn * tiles + step], recv_sem=rows_recv.at[part, turn * tiles + step],
            device_id=where, device_id_type=MESH,
        )

    def when_direct(act):
        def body(turn, step):
            if relay and turn in (1, groups - 1):
                pl.when(group_id != (groups - 1 if turn == 1 else 0))(lambda: act(turn, step))
            else:
                act(turn, step)

        others(body)

    def relay_copy(part, step):
        far = jnp.where(group_id == 1, groups - 1, 0)
        slot = far * tiles + lax.rem(tile_id - step + tiles, tiles)
        end = jnp.where(group_id == 1, 0, groups - 1)
        arrival = jnp.where(group_id == 1, 1, groups - 1) * tiles + step
        return pltpu.make_async_remote_copy(
            src_ref=all_rows.at[slot, :, spans[part]], dst_ref=all_rows.at[slot, :, spans[part]],
            send_sem=relay_send.at[part, step], recv_sem=rows_recv.at[part, arrival],
            device_id={"pulse": end, "tile": tile_id}, device_id_type=MESH,
        )

    last = []
    for part, (start, stop) in enumerate(parts):
        if tiles == TILE_GROUP:
            if part == 0:
                gather(0)
            last = steer(0, start, stop, last)
        else:
            each(tiles // TILE_GROUP, lambda pair: (gather(pair), steer(pair, start, stop, [])))
        when_direct(lambda turn, step: rows_copy(part, turn, step).start())
    keep_own = pltpu.make_async_copy(own_rows.at[tile_id], all_rows.at[me], own_sem)
    keep_own.start()

    others(lambda turn, step: bins_copy(turn, step).wait_recv())
    azimuth_total = AZ_DEV * members
    norm_scale = (pulses * members) ** (-0.5)
    per_member = 2 * pulses
    per_chunk = LANES // per_member
    first_line = tile_id * (groups * AZ_DEV) + group_id * AZ_DEV
    az_line = first_line + lax.broadcasted_iota(jnp.int32, (AZ_DEV, LANES), 0)
    az_lane = lax.broadcasted_iota(jnp.int32, (AZ_DEV, LANES), 1)
    is_imag = (az_lane // pulses) % 2 == 1
    for chunk in range(members // per_chunk):
        known = jnp.zeros((8, LANES), jnp.int32)
        for at in range(per_chunk):
            known = jnp.where(lane // per_member == at, all_bins[chunk * per_chunk + at], known)
        angle = wrap(az_line * known[0:1, :], azimuth_total).astype(jnp.float32) * (2.0 * math.pi / azimuth_total)
        weight = known[1:2, :].astype(jnp.float32) * norm_scale
        factor_re = jnp.cos(angle) * weight
        factor_im = jnp.sin(angle) * weight
        factor_ref[:, chunk * LANES:(chunk + 1) * LANES] = jnp.concatenate(
            [jnp.where(is_imag, -factor_im, factor_re), jnp.where(is_imag, factor_re, factor_im)], axis=0
        ).astype(jnp.bfloat16)

    if relay:
        for part in range(len(parts)):
            others(lambda turn, step: rows_copy(part, turn, step).wait_recv(), [2])

            @pl.when(relays)
            def _():
                each(tiles, lambda step: relay_copy(part, step).start())

    for part in range(len(parts)):
        rest = [turn for turn in turns if not (relay and turn == 2)]
        others(lambda turn, step: rows_copy(part, turn, step).wait_recv(), rest)
    keep_own.wait()

    @pl.when(range_id > 0)
    def _():
        to_left.wait_send()

    @pl.when(range_id < ranges - 1)
    def _():
        to_right.wait_send()

    others(lambda turn, step: bins_copy(turn, step).wait_send())
    for part in range(len(parts)):
        when_direct(lambda turn, step: rows_copy(part, turn, step).wait_send())
    if relay:

        @pl.when(relays)
        def _():
            for part in range(len(parts)):
                each(tiles, lambda step: relay_copy(part, step).wait_send())


def local(echo, replica, interp, band_start, visible, doppler, range_step):
    chirp_blocks = replica.shape[1] // LANES
    pulses = echo.shape[1]
    samples = echo.shape[2]
    samp_blocks = samples // LANES
    lines = interp.shape[0] * interp.shape[2]
    band_blocks = interp.shape[0] + 1
    tiles = lax.axis_size("tile")
    groups = lax.axis_size("pulse")
    ranges = lax.axis_size("range")
    members = tiles * groups
    half = chirp_blocks * LANES // 2
    rows = TILE_GROUP * pulses
    seen_pad = -(-(band_blocks + chirp_blocks) // 8) * 8
    ext_blocks = samp_blocks + chirp_blocks + 8
    sizes = (pulses, tiles, groups, ranges, band_blocks, chirp_blocks, samp_blocks, lines)
    hbm = pl.BlockSpec(memory_space=pl.ANY)
    vmem = pl.BlockSpec(memory_space=pltpu.VMEM)
    rows_out, factors = pl.pallas_call(
        functools.partial(image_kernel, sizes),
        out_shape=(
            jax.ShapeDtypeStruct((members, 2 * pulses, lines), jnp.bfloat16),
            jax.ShapeDtypeStruct((2 * AZ_DEV, members * 2 * pulses), jnp.bfloat16),
        ),
        in_specs=[hbm] * 7,
        out_specs=(hbm, vmem),
        scratch_shapes=[
            pltpu.SMEM((tiles, 1, pulses), jnp.int32),
            pltpu.SMEM((tiles, pulses), jnp.int32),
            pltpu.SMEM((pulses,), jnp.int32),
            pltpu.SMEM((pulses,), jnp.int32),
            pltpu.VMEM((2 * pulses, samples), jnp.bfloat16),
            pltpu.VMEM(replica.shape, jnp.bfloat16),
            pltpu.VMEM(interp.shape, jnp.bfloat16),
            pltpu.SemaphoreType.DMA((7,)),
            pltpu.VMEM((2 * pulses, half), jnp.bfloat16),
            pltpu.VMEM((2 * pulses, half), jnp.bfloat16),
            pltpu.VMEM((ext_blocks * pulses, LANES), jnp.float32),
            pltpu.VMEM((ext_blocks * pulses, LANES), jnp.float32),
            pltpu.VMEM((seen_pad * rows, LANES), jnp.float32),
            pltpu.VMEM((seen_pad * rows, LANES), jnp.float32),
            pltpu.VMEM((seen_pad * rows, 2 * LANES), jnp.bfloat16),
            pltpu.VMEM((chirp_blocks + 1, 2 * LANES, 2 * LANES), jnp.bfloat16),
            pltpu.VMEM((pulses, lines), jnp.float32),
            pltpu.VMEM((pulses, lines), jnp.float32),
            pltpu.VMEM((tiles, 8, LANES), jnp.int32),
            pltpu.VMEM((members, 8, LANES), jnp.int32),
            pltpu.VMEM((tiles, 2 * pulses, lines), jnp.bfloat16),
            pltpu.SemaphoreType.DMA,
            pltpu.SemaphoreType.DMA((2,)),
            pltpu.SemaphoreType.DMA((2,)),
            pltpu.SemaphoreType.DMA((members,)),
            pltpu.SemaphoreType.DMA((members,)),
            pltpu.SemaphoreType.DMA((2, members)),
            pltpu.SemaphoreType.DMA((2, members)),
            pltpu.SemaphoreType.DMA((2, tiles)),
        ],
        compiler_params=pltpu.CompilerParams(
            collective_id=0, has_side_effects=True, vmem_limit_bytes=60 * 1024 * 1024
        ),
        name="backproject",
    )(
        band_start.transpose(1, 2, 0), visible.T, doppler, range_step,
        echo.reshape(2 * pulses, samples), replica, interp,
    )
    image = jnp.dot(
        factors, rows_out.reshape(members * 2 * pulses, lines), preferred_element_type=jnp.float32
    )
    return image.reshape(2, AZ_DEV, lines)


def solution(mesh):
    in_specs = (
        P(None, ("pulse", "tile"), "range"),
        P(),
        P("range", None, None),
        P(("pulse", "tile"), None, "range"),
        P(("pulse", "tile"), None),
        P(("pulse", "tile")),
        P(("pulse", "tile")),
    )
    out_specs = P(None, ("tile", "pulse"), "range")
    return jax.shard_map(local, mesh=mesh, in_specs=in_specs, out_specs=out_specs, check_vma=False)
```

```python
import functools
import math

import jax
import jax.numpy as jnp
from jax import lax
from jax.experimental import pallas as pl
from jax.experimental.pallas import tpu as pltpu
from jax.sharding import PartitionSpec as P

AZ_DEV = 64
LANES = 128
TILE_GROUP = 2
MESH = pl.DeviceIdType.MESH


def each(count, body, first=0):
    if count <= 16:
        for step in range(first, count):
            body(step)
    else:
        lax.fori_loop(first, count, lambda step, carry: (body(step), carry)[1], 0)


def wrap(value, total):
    if total & (total - 1) == 0:
        return value & (total - 1)
    return lax.rem(value, jnp.int32(total))


def image_kernel(
    sizes,
    starts_in, visible_in, doppler_in, step_in,
    echo_in, replica_in, interp_in,
    all_rows, factor_ref,
    starts_ref, visible_ref, doppler_ref, step_ref,
    echo_ref, replica_ref, interp_ref, load_sem,
    left_halo, right_halo, ext_re, ext_im, gat_re, gat_im, gat, chirp,
    turn_cos, turn_sin, own_bins, all_bins, own_rows, own_sem,
    halo_send, halo_recv, bins_send, bins_recv, rows_send, rows_recv, relay_send,
):
    pulses, tiles, groups, ranges, band_blocks, chirp_blocks, samp_blocks, lines = sizes
    half_blocks = chirp_blocks // 2
    half = half_blocks * LANES
    samples = samp_blocks * LANES
    members = groups * tiles
    seen_blocks = band_blocks + chirp_blocks
    seen_pad = gat_re.shape[0] // (TILE_GROUP * pulses)
    group_id = lax.axis_index("pulse")
    tile_id = lax.axis_index("tile")
    range_id = lax.axis_index("range")
    me = group_id * tiles + tile_id

    turns = [2 % groups] + [turn for turn in range(1, groups) if turn != 2 % groups] + [0]

    def others(body, which=None):
        for turn in turns if which is None else which:
            each(tiles, functools.partial(body, turn), first=1 if turn == 0 else 0)

    def member(turn, step):
        group = lax.rem(group_id + turn, groups)
        tile = lax.rem(tile_id + step, tiles)
        return tile, {"pulse": group, "tile": tile}

    places = (
        (step_in, step_ref), (doppler_in, doppler_ref), (visible_in, visible_ref), (starts_in, starts_ref),
        (replica_in, replica_ref), (echo_in, echo_ref), (interp_in, interp_ref),
    )
    loads = [
        pltpu.make_async_copy(there, here, load_sem.at[place]) for place, (there, here) in enumerate(places)
    ]
    load_step, load_doppler, load_visible, load_starts, load_replica, load_echo, load_interp = loads
    for load in loads:
        load.start()

    barrier = pltpu.get_barrier_semaphore()

    @pl.when(range_id > 0)
    def _():
        pl.semaphore_signal(barrier, inc=1, device_id={"range": range_id - 1}, device_id_type=MESH)

    @pl.when(range_id < ranges - 1)
    def _():
        pl.semaphore_signal(barrier, inc=1, device_id={"range": range_id + 1}, device_id_type=MESH)

    def greet(turn, step):
        _, where = member(turn, step)
        pl.semaphore_signal(barrier, inc=1, device_id=where, device_id_type=MESH)

    others(greet)
    load_step.wait()
    line_number = range_id * lines + lax.broadcasted_iota(jnp.int32, (pulses, lines), 1)
    pulse_row = lax.broadcasted_iota(jnp.int32, (pulses, lines), 0)
    steps = jnp.zeros((pulses, lines), jnp.int32)
    for q in range(pulses):
        steps = jnp.where(pulse_row == q, step_ref[q], steps)
    range_total = lines * ranges
    angle = wrap(steps * line_number, range_total).astype(jnp.float32) * (2.0 * math.pi / range_total)
    turn_cos[...] = jnp.cos(angle)
    turn_sin[...] = jnp.sin(angle)

    neighbours = (range_id > 0).astype(jnp.int32) + (range_id < ranges - 1).astype(jnp.int32)
    pl.semaphore_wait(barrier, members - 1 + neighbours)

    to_left = pltpu.make_async_remote_copy(
        src_ref=echo_in.at[:, pl.ds(0, half)], dst_ref=right_halo,
        send_sem=halo_send.at[0], recv_sem=halo_recv.at[0],
        device_id={"range": lax.max(range_id - 1, 0)}, device_id_type=MESH,
    )
    to_right = pltpu.make_async_remote_copy(
        src_ref=echo_in.at[:, pl.ds(samples - half, half)], dst_ref=left_halo,
        send_sem=halo_send.at[1], recv_sem=halo_recv.at[1],
        device_id={"range": lax.min(range_id + 1, ranges - 1)}, device_id_type=MESH,
    )

    @pl.when(range_id > 0)
    def _():
        to_left.start()

    @pl.when(range_id < ranges - 1)
    def _():
        to_right.start()

    load_doppler.wait()
    load_visible.wait()
    load_starts.wait()
    lane = lax.broadcasted_iota(jnp.int32, (8, LANES), 1)
    row = lax.broadcasted_iota(jnp.int32, (8, LANES), 0)
    lane_pulse = lane % pulses
    bins = jnp.zeros((8, LANES), jnp.int32)
    for q in range(pulses):
        bins = jnp.where(lane_pulse == q, doppler_ref[q], bins)

    def fill_bins(tile):
        flags = jnp.zeros((8, LANES), jnp.int32)
        for q in range(pulses):
            flags = jnp.where(lane_pulse == q, visible_ref[tile, q], flags)
        own_bins[tile] = jnp.where(row == 0, bins, flags)

    each(tiles, fill_bins)

    def bins_copy(turn, step):
        tile, where = member(turn, step)
        return pltpu.make_async_remote_copy(
            src_ref=own_bins.at[tile], dst_ref=all_bins.at[me],
            send_sem=bins_send.at[turn * tiles + step], recv_sem=bins_recv.at[turn * tiles + step],
            device_id=where, device_id_type=MESH,
        )

    others(lambda turn, step: bins_copy(turn, step).start())
    all_bins[me] = own_bins[tile_id]

    load_replica.wait()

    wide = chirp_blocks + 1
    taps = replica_ref[...]
    flip = (
        lax.broadcasted_iota(jnp.int32, (LANES, LANES), 0)
        + lax.broadcasted_iota(jnp.int32, (LANES, LANES), 1) == LANES - 1
    ).astype(jnp.bfloat16)
    by_block = jnp.concatenate([taps[:, block * LANES:(block + 1) * LANES] for block in range(chirp_blocks)], axis=0)
    flipped = jnp.dot(by_block, flip, preferred_element_type=jnp.float32)

    def shifted(part):
        pieces = [flipped[2 * block + part:2 * block + part + 1] for block in reversed(range(chirp_blocks))]
        line = jnp.concatenate([jnp.zeros((1, LANES), jnp.float32)] + pieces, axis=1)
        spread = jnp.broadcast_to(line, (LANES, wide * LANES))
        moved = pltpu.roll(spread, 1, 1, stride=1, stride_axis=0).astype(jnp.bfloat16)
        places = [(wide - turn) % wide for turn in range(wide)]
        return [moved[:, place * LANES:(place + 1) * LANES] for place in places]

    for turn, block in enumerate(shifted(0)):
        chirp[turn, :LANES, :LANES] = block
        chirp[turn, LANES:, LANES:] = block
    for turn, block in enumerate(shifted(1)):
        chirp[turn, LANES:, :LANES] = block
        chirp[turn, :LANES, LANES:] = -block

    def lay(block, values):
        ext_re[block * pulses:(block + 1) * pulses, :] = values[:pulses]
        ext_im[block * pulses:(block + 1) * pulses, :] = values[pulses:]

    load_echo.wait()
    for block in range(samp_blocks):
        lay(half_blocks + block, echo_ref[:, block * LANES:(block + 1) * LANES].astype(jnp.float32))
    filled = samp_blocks + 2 * half_blocks
    tail = ext_re.shape[0] - filled * pulses
    ext_re[filled * pulses:, :] = jnp.zeros((tail, LANES), jnp.float32)
    ext_im[filled * pulses:, :] = jnp.zeros((tail, LANES), jnp.float32)

    @pl.when(range_id > 0)
    def _():
        to_right.wait_recv()

    @pl.when(range_id == 0)
    def _():
        left_halo[...] = jnp.zeros_like(left_halo)

    @pl.when(range_id < ranges - 1)
    def _():
        to_left.wait_recv()

    @pl.when(range_id == ranges - 1)
    def _():
        right_halo[...] = jnp.zeros_like(right_halo)

    for block in range(half_blocks):
        lay(block, left_halo[:, block * LANES:(block + 1) * LANES].astype(jnp.float32))
        lay(
            half_blocks + samp_blocks + block,
            right_halo[:, block * LANES:(block + 1) * LANES].astype(jnp.float32),
        )

    load_interp.wait()

    rows = TILE_GROUP * pulses
    cut = band_blocks // 2 + 1
    parts = [(0, band_blocks)]
    spans = [
        pl.ds(max(start - 1, 0) * LANES, (stop - 1 - max(start - 1, 0)) * LANES) for start, stop in parts
    ]

    def gather(pair):
        for which in range(TILE_GROUP):
            for q in range(pulses):
                first = starts_ref[pair * TILE_GROUP + which, 0, q] // LANES
                source = pl.ds(first * pulses + q, seen_pad, stride=pulses)
                target = pl.ds(which * pulses + q, seen_pad, stride=rows)
                gat_re[target, :] = ext_re[source, :]
                gat_im[target, :] = ext_im[source, :]
        gat[:, :LANES] = gat_re[...].astype(jnp.bfloat16)
        gat[:, LANES:] = gat_im[...].astype(jnp.bfloat16)

    def steer(pair, start, stop, before):
        total = jnp.zeros(((stop - start) * rows, 2 * LANES), jnp.float32)
        for turn in range(chirp_blocks + 1):
            total = total + lax.dot_general(
                gat[(turn + start) * rows:(turn + stop) * rows, :], chirp[turn],
                (((1,), (0,)), ((), ())), preferred_element_type=jnp.float32,
            )
        made = total.astype(jnp.bfloat16)
        bands = before + [made[j * rows:(j + 1) * rows] for j in range(stop - start)]
        for here, after, j in zip(bands, bands[1:], range(start - len(before), stop - 1)):
            window = jnp.concatenate(
                [
                    jnp.concatenate([here[:, :LANES], after[:, :LANES]], axis=1),
                    jnp.concatenate([here[:, LANES:], after[:, LANES:]], axis=1),
                ],
                axis=0,
            )
            values = jnp.dot(window, interp_ref[j], preferred_element_type=jnp.float32)
            cosine = turn_cos[:, j * LANES:(j + 1) * LANES]
            sine = turn_sin[:, j * LANES:(j + 1) * LANES]
            for which in range(TILE_GROUP):
                real = values[which * pulses:(which + 1) * pulses]
                imag = values[rows + which * pulses:rows + (which + 1) * pulses]
                steered = jnp.concatenate(
                    [real * cosine - imag * sine, real * sine + imag * cosine], axis=0
                )
                own_rows[pair * TILE_GROUP + which, :, j * LANES:(j + 1) * LANES] = steered.astype(jnp.bfloat16)
        return bands[-1:]

    relay = False
    relays = jnp.logical_or(group_id == 1, group_id == groups - 2)

    def rows_copy(part, turn, step):
        tile, where = member(turn, step)
        return pltpu.make_async_remote_copy(
            src_ref=own_rows.at[tile, :, spans[part]], dst_ref=all_rows.at[me, :, spans[part]],
            send_sem=rows_send.at[part, turn * tiles + step], recv_sem=rows_recv.at[part, turn * tiles + step],
            device_id=where, device_id_type=MESH,
        )

    def when_direct(act):
        def body(turn, step):
            if relay and turn in (1, groups - 1):
                pl.when(group_id != (groups - 1 if turn == 1 else 0))(lambda: act(turn, step))
            else:
                act(turn, step)

        others(body)

    def relay_copy(part, step):
        far = jnp.where(group_id == 1, groups - 1, 0)
        slot = far * tiles + lax.rem(tile_id - step + tiles, tiles)
        end = jnp.where(group_id == 1, 0, groups - 1)
        arrival = jnp.where(group_id == 1, 1, groups - 1) * tiles + step
        return pltpu.make_async_remote_copy(
            src_ref=all_rows.at[slot, :, spans[part]], dst_ref=all_rows.at[slot, :, spans[part]],
            send_sem=relay_send.at[part, step], recv_sem=rows_recv.at[part, arrival],
            device_id={"pulse": end, "tile": tile_id}, device_id_type=MESH,
        )

    last = []
    for part, (start, stop) in enumerate(parts):
        if tiles == TILE_GROUP:
            if part == 0:
                gather(0)
            last = steer(0, start, stop, last)
        else:
            each(tiles // TILE_GROUP, lambda pair: (gather(pair), steer(pair, start, stop, [])))
        when_direct(lambda turn, step: rows_copy(part, turn, step).start())
    keep_own = pltpu.make_async_copy(own_rows.at[tile_id], all_rows.at[me], own_sem)
    keep_own.start()

    others(lambda turn, step: bins_copy(turn, step).wait_recv())
    azimuth_total = AZ_DEV * members
    norm_scale = (pulses * members) ** (-0.5)
    per_member = 2 * pulses
    per_chunk = LANES // per_member
    first_line = tile_id * (groups * AZ_DEV) + group_id * AZ_DEV
    az_line = first_line + lax.broadcasted_iota(jnp.int32, (AZ_DEV, LANES), 0)
    az_lane = lax.broadcasted_iota(jnp.int32, (AZ_DEV, LANES), 1)
    is_imag = (az_lane // pulses) % 2 == 1
    for chunk in range(members // per_chunk):
        known = jnp.zeros((8, LANES), jnp.int32)
        for at in range(per_chunk):
            known = jnp.where(lane // per_member == at, all_bins[chunk * per_chunk + at], known)
        angle = wrap(az_line * known[0:1, :], azimuth_total).astype(jnp.float32) * (2.0 * math.pi / azimuth_total)
        weight = known[1:2, :].astype(jnp.float32) * norm_scale
        factor_re = jnp.cos(angle) * weight
        factor_im = jnp.sin(angle) * weight
        factor_ref[:, chunk * LANES:(chunk + 1) * LANES] = jnp.concatenate(
            [jnp.where(is_imag, -factor_im, factor_re), jnp.where(is_imag, factor_re, factor_im)], axis=0
        ).astype(jnp.bfloat16)

    if relay:
        for part in range(len(parts)):
            others(lambda turn, step: rows_copy(part, turn, step).wait_recv(), [2])

            @pl.when(relays)
            def _():
                each(tiles, lambda step: relay_copy(part, step).start())

    for part in range(len(parts)):
        rest = [turn for turn in turns if not (relay and turn == 2)]
        others(lambda turn, step: rows_copy(part, turn, step).wait_recv(), rest)
    keep_own.wait()

    @pl.when(range_id > 0)
    def _():
        to_left.wait_send()

    @pl.when(range_id < ranges - 1)
    def _():
        to_right.wait_send()

    others(lambda turn, step: bins_copy(turn, step).wait_send())
    for part in range(len(parts)):
        when_direct(lambda turn, step: rows_copy(part, turn, step).wait_send())
    if relay:

        @pl.when(relays)
        def _():
            for part in range(len(parts)):
                each(tiles, lambda step: relay_copy(part, step).wait_send())


def local(echo, replica, interp, band_start, visible, doppler, range_step):
    chirp_blocks = replica.shape[1] // LANES
    pulses = echo.shape[1]
    samples = echo.shape[2]
    samp_blocks = samples // LANES
    lines = interp.shape[0] * interp.shape[2]
    band_blocks = interp.shape[0] + 1
    tiles = lax.axis_size("tile")
    groups = lax.axis_size("pulse")
    ranges = lax.axis_size("range")
    members = tiles * groups
    half = chirp_blocks * LANES // 2
    rows = TILE_GROUP * pulses
    seen_pad = -(-(band_blocks + chirp_blocks) // 8) * 8
    ext_blocks = samp_blocks + chirp_blocks + 8
    sizes = (pulses, tiles, groups, ranges, band_blocks, chirp_blocks, samp_blocks, lines)
    hbm = pl.BlockSpec(memory_space=pl.ANY)
    vmem = pl.BlockSpec(memory_space=pltpu.VMEM)
    rows_out, factors = pl.pallas_call(
        functools.partial(image_kernel, sizes),
        out_shape=(
            jax.ShapeDtypeStruct((members, 2 * pulses, lines), jnp.bfloat16),
            jax.ShapeDtypeStruct((2 * AZ_DEV, members * 2 * pulses), jnp.bfloat16),
        ),
        in_specs=[hbm] * 7,
        out_specs=(hbm, vmem),
        scratch_shapes=[
            pltpu.SMEM((tiles, 1, pulses), jnp.int32),
            pltpu.SMEM((tiles, pulses), jnp.int32),
            pltpu.SMEM((pulses,), jnp.int32),
            pltpu.SMEM((pulses,), jnp.int32),
            pltpu.VMEM((2 * pulses, samples), jnp.bfloat16),
            pltpu.VMEM(replica.shape, jnp.bfloat16),
            pltpu.VMEM(interp.shape, jnp.bfloat16),
            pltpu.SemaphoreType.DMA((7,)),
            pltpu.VMEM((2 * pulses, half), jnp.bfloat16),
            pltpu.VMEM((2 * pulses, half), jnp.bfloat16),
            pltpu.VMEM((ext_blocks * pulses, LANES), jnp.float32),
            pltpu.VMEM((ext_blocks * pulses, LANES), jnp.float32),
            pltpu.VMEM((seen_pad * rows, LANES), jnp.float32),
            pltpu.VMEM((seen_pad * rows, LANES), jnp.float32),
            pltpu.VMEM((seen_pad * rows, 2 * LANES), jnp.bfloat16),
            pltpu.VMEM((chirp_blocks + 1, 2 * LANES, 2 * LANES), jnp.bfloat16),
            pltpu.VMEM((pulses, lines), jnp.float32),
            pltpu.VMEM((pulses, lines), jnp.float32),
            pltpu.VMEM((tiles, 8, LANES), jnp.int32),
            pltpu.VMEM((members, 8, LANES), jnp.int32),
            pltpu.VMEM((tiles, 2 * pulses, lines), jnp.bfloat16),
            pltpu.SemaphoreType.DMA,
            pltpu.SemaphoreType.DMA((2,)),
            pltpu.SemaphoreType.DMA((2,)),
            pltpu.SemaphoreType.DMA((members,)),
            pltpu.SemaphoreType.DMA((members,)),
            pltpu.SemaphoreType.DMA((2, members)),
            pltpu.SemaphoreType.DMA((2, members)),
            pltpu.SemaphoreType.DMA((2, tiles)),
        ],
        compiler_params=pltpu.CompilerParams(
            collective_id=0, has_side_effects=True, vmem_limit_bytes=60 * 1024 * 1024
        ),
        name="backproject",
    )(
        band_start.transpose(1, 2, 0), visible.T, doppler, range_step,
        echo.reshape(2 * pulses, samples), replica, interp,
    )
    image = jnp.dot(
        factors, rows_out.reshape(members * 2 * pulses, lines), preferred_element_type=jnp.float32
    )
    return image.reshape(2, AZ_DEV, lines)


def solution(mesh):
    in_specs = (
        P(None, ("pulse", "tile"), "range"),
        P(),
        P("range", None, None),
        P(("pulse", "tile"), None, "range"),
        P(("pulse", "tile"), None),
        P(("pulse", "tile")),
        P(("pulse", "tile")),
    )
    out_specs = P(None, ("tile", "pulse"), "range")
    return jax.shard_map(local, mesh=mesh, in_specs=in_specs, out_specs=out_specs, check_vma=False)
```

```python
import functools
import math

import jax
import jax.numpy as jnp
from jax import lax
from jax.experimental import pallas as pl
from jax.experimental.pallas import tpu as pltpu
from jax.sharding import PartitionSpec as P

AZ_DEV = 64
LANES = 128
TILE_GROUP = 2
MESH = pl.DeviceIdType.MESH


def each(count, body, first=0):
    if count <= 16:
        for step in range(first, count):
            body(step)
    else:
        lax.fori_loop(first, count, lambda step, carry: (body(step), carry)[1], 0)


def wrap(value, total):
    if total & (total - 1) == 0:
        return value & (total - 1)
    return lax.rem(value, jnp.int32(total))


def image_kernel(
    sizes,
    starts_in, visible_in, doppler_in, step_in,
    echo_in, replica_in, interp_in,
    all_rows, factor_ref,
    starts_ref, visible_ref, doppler_ref, step_ref,
    echo_ref, replica_ref, interp_ref, load_sem,
    left_halo, right_halo, ext_re, ext_im, gat_re, gat_im, gat, chirp,
    turn_cos, turn_sin, own_bins, all_bins, own_rows, own_sem,
    halo_send, halo_recv, bins_send, bins_recv, rows_send, rows_recv, relay_send,
):
    pulses, tiles, groups, ranges, band_blocks, chirp_blocks, samp_blocks, lines = sizes
    half_blocks = chirp_blocks // 2
    half = half_blocks * LANES
    samples = samp_blocks * LANES
    members = groups * tiles
    seen_blocks = band_blocks + chirp_blocks
    seen_pad = gat_re.shape[0] // (TILE_GROUP * pulses)
    group_id = lax.axis_index("pulse")
    tile_id = lax.axis_index("tile")
    range_id = lax.axis_index("range")
    me = group_id * tiles + tile_id

    turns = [2 % groups] + [turn for turn in range(1, groups) if turn != 2 % groups] + [0]

    def others(body, which=None):
        for turn in turns if which is None else which:
            each(tiles, functools.partial(body, turn), first=1 if turn == 0 else 0)

    def member(turn, step):
        group = lax.rem(group_id + turn, groups)
        tile = lax.rem(tile_id + step, tiles)
        return tile, {"pulse": group, "tile": tile}

    places = (
        (step_in, step_ref), (doppler_in, doppler_ref), (visible_in, visible_ref), (starts_in, starts_ref),
        (replica_in, replica_ref), (echo_in, echo_ref), (interp_in, interp_ref),
    )
    loads = [
        pltpu.make_async_copy(there, here, load_sem.at[place]) for place, (there, here) in enumerate(places)
    ]
    load_step, load_doppler, load_visible, load_starts, load_replica, load_echo, load_interp = loads
    for load in loads:
        load.start()

    barrier = pltpu.get_barrier_semaphore()

    @pl.when(range_id > 0)
    def _():
        pl.semaphore_signal(barrier, inc=1, device_id={"range": range_id - 1}, device_id_type=MESH)

    @pl.when(range_id < ranges - 1)
    def _():
        pl.semaphore_signal(barrier, inc=1, device_id={"range": range_id + 1}, device_id_type=MESH)

    def greet(turn, step):
        _, where = member(turn, step)
        pl.semaphore_signal(barrier, inc=1, device_id=where, device_id_type=MESH)

    others(greet)
    load_step.wait()
    line_number = range_id * lines + lax.broadcasted_iota(jnp.int32, (pulses, lines), 1)
    pulse_row = lax.broadcasted_iota(jnp.int32, (pulses, lines), 0)
    steps = jnp.zeros((pulses, lines), jnp.int32)
    for q in range(pulses):
        steps = jnp.where(pulse_row == q, step_ref[q], steps)
    range_total = lines * ranges
    angle = wrap(steps * line_number, range_total).astype(jnp.float32) * (2.0 * math.pi / range_total)
    turn_cos[...] = jnp.cos(angle)
    turn_sin[...] = jnp.sin(angle)

    neighbours = (range_id > 0).astype(jnp.int32) + (range_id < ranges - 1).astype(jnp.int32)
    pl.semaphore_wait(barrier, members - 1 + neighbours)

    to_left = pltpu.make_async_remote_copy(
        src_ref=echo_in.at[:, pl.ds(0, half)], dst_ref=right_halo,
        send_sem=halo_send.at[0], recv_sem=halo_recv.at[0],
        device_id={"range": lax.max(range_id - 1, 0)}, device_id_type=MESH,
    )
    to_right = pltpu.make_async_remote_copy(
        src_ref=echo_in.at[:, pl.ds(samples - half, half)], dst_ref=left_halo,
        send_sem=halo_send.at[1], recv_sem=halo_recv.at[1],
        device_id={"range": lax.min(range_id + 1, ranges - 1)}, device_id_type=MESH,
    )

    @pl.when(range_id > 0)
    def _():
        to_left.start()

    @pl.when(range_id < ranges - 1)
    def _():
        to_right.start()

    load_doppler.wait()
    load_visible.wait()
    load_starts.wait()
    lane = lax.broadcasted_iota(jnp.int32, (8, LANES), 1)
    row = lax.broadcasted_iota(jnp.int32, (8, LANES), 0)
    lane_pulse = lane % pulses
    bins = jnp.zeros((8, LANES), jnp.int32)
    for q in range(pulses):
        bins = jnp.where(lane_pulse == q, doppler_ref[q], bins)

    def fill_bins(tile):
        flags = jnp.zeros((8, LANES), jnp.int32)
        for q in range(pulses):
            flags = jnp.where(lane_pulse == q, visible_ref[tile, q], flags)
        own_bins[tile] = jnp.where(row == 0, bins, flags)

    each(tiles, fill_bins)

    def bins_copy(turn, step):
        tile, where = member(turn, step)
        return pltpu.make_async_remote_copy(
            src_ref=own_bins.at[tile], dst_ref=all_bins.at[me],
            send_sem=bins_send.at[turn * tiles + step], recv_sem=bins_recv.at[turn * tiles + step],
            device_id=where, device_id_type=MESH,
        )

    others(lambda turn, step: bins_copy(turn, step).start())
    all_bins[me] = own_bins[tile_id]

    load_replica.wait()

    wide = chirp_blocks + 1
    taps = replica_ref[...]
    flip = (
        lax.broadcasted_iota(jnp.int32, (LANES, LANES), 0)
        + lax.broadcasted_iota(jnp.int32, (LANES, LANES), 1) == LANES - 1
    ).astype(jnp.bfloat16)
    by_block = jnp.concatenate([taps[:, block * LANES:(block + 1) * LANES] for block in range(chirp_blocks)], axis=0)
    flipped = jnp.dot(by_block, flip, preferred_element_type=jnp.float32)

    def shifted(part):
        pieces = [flipped[2 * block + part:2 * block + part + 1] for block in reversed(range(chirp_blocks))]
        line = jnp.concatenate([jnp.zeros((1, LANES), jnp.float32)] + pieces, axis=1)
        spread = jnp.broadcast_to(line, (LANES, wide * LANES))
        moved = pltpu.roll(spread, 1, 1, stride=1, stride_axis=0).astype(jnp.bfloat16)
        places = [(wide - turn) % wide for turn in range(wide)]
        return [moved[:, place * LANES:(place + 1) * LANES] for place in places]

    for turn, block in enumerate(shifted(0)):
        chirp[turn, :LANES, :LANES] = block
        chirp[turn, LANES:, LANES:] = block
    for turn, block in enumerate(shifted(1)):
        chirp[turn, LANES:, :LANES] = block
        chirp[turn, :LANES, LANES:] = -block

    def lay(block, values):
        ext_re[block * pulses:(block + 1) * pulses, :] = values[:pulses]
        ext_im[block * pulses:(block + 1) * pulses, :] = values[pulses:]

    load_echo.wait()
    for block in range(samp_blocks):
        lay(half_blocks + block, echo_ref[:, block * LANES:(block + 1) * LANES].astype(jnp.float32))
    filled = samp_blocks + 2 * half_blocks
    tail = ext_re.shape[0] - filled * pulses
    ext_re[filled * pulses:, :] = jnp.zeros((tail, LANES), jnp.float32)
    ext_im[filled * pulses:, :] = jnp.zeros((tail, LANES), jnp.float32)

    @pl.when(range_id > 0)
    def _():
        to_right.wait_recv()

    @pl.when(range_id == 0)
    def _():
        left_halo[...] = jnp.zeros_like(left_halo)

    @pl.when(range_id < ranges - 1)
    def _():
        to_left.wait_recv()

    @pl.when(range_id == ranges - 1)
    def _():
        right_halo[...] = jnp.zeros_like(right_halo)

    for block in range(half_blocks):
        lay(block, left_halo[:, block * LANES:(block + 1) * LANES].astype(jnp.float32))
        lay(
            half_blocks + samp_blocks + block,
            right_halo[:, block * LANES:(block + 1) * LANES].astype(jnp.float32),
        )

    load_interp.wait()

    rows = TILE_GROUP * pulses
    cut = band_blocks // 2 + 1
    parts = [(0, band_blocks)]
    spans = [
        pl.ds(max(start - 1, 0) * LANES, (stop - 1 - max(start - 1, 0)) * LANES) for start, stop in parts
    ]

    def gather(pair):
        for which in range(TILE_GROUP):
            for q in range(pulses):
                first = starts_ref[pair * TILE_GROUP + which, 0, q] // LANES
                source = pl.ds(first * pulses + q, seen_pad, stride=pulses)
                target = pl.ds(which * pulses + q, seen_pad, stride=rows)
                gat_re[target, :] = ext_re[source, :]
                gat_im[target, :] = ext_im[source, :]
        gat[:, :LANES] = gat_re[...].astype(jnp.bfloat16)
        gat[:, LANES:] = gat_im[...].astype(jnp.bfloat16)

    def steer(pair, start, stop, before):
        total = jnp.zeros(((stop - start) * rows, 2 * LANES), jnp.float32)
        for turn in range(chirp_blocks + 1):
            total = total + lax.dot_general(
                gat[(turn + start) * rows:(turn + stop) * rows, :], chirp[turn],
                (((1,), (0,)), ((), ())), preferred_element_type=jnp.float32,
            )
        made = total.astype(jnp.bfloat16)
        bands = before + [made[j * rows:(j + 1) * rows] for j in range(stop - start)]
        for here, after, j in zip(bands, bands[1:], range(start - len(before), stop - 1)):
            window = jnp.concatenate(
                [
                    jnp.concatenate([here[:, :LANES], after[:, :LANES]], axis=1),
                    jnp.concatenate([here[:, LANES:], after[:, LANES:]], axis=1),
                ],
                axis=0,
            )
            values = jnp.dot(window, interp_ref[j], preferred_element_type=jnp.float32)
            cosine = turn_cos[:, j * LANES:(j + 1) * LANES]
            sine = turn_sin[:, j * LANES:(j + 1) * LANES]
            for which in range(TILE_GROUP):
                real = values[which * pulses:(which + 1) * pulses]
                imag = values[rows + which * pulses:rows + (which + 1) * pulses]
                steered = jnp.concatenate(
                    [real * cosine - imag * sine, real * sine + imag * cosine], axis=0
                )
                own_rows[pair * TILE_GROUP + which, :, j * LANES:(j + 1) * LANES] = steered.astype(jnp.bfloat16)
        return bands[-1:]

    relay = groups == 4
    relays = jnp.logical_or(group_id == 1, group_id == groups - 2)

    def rows_copy(part, turn, step):
        tile, where = member(turn, step)
        return pltpu.make_async_remote_copy(
            src_ref=own_rows.at[tile, :, spans[part]], dst_ref=all_rows.at[me, :, spans[part]],
            send_sem=rows_send.at[part, turn * tiles + step], recv_sem=rows_recv.at[part, turn * tiles + step],
            device_id=where, device_id_type=MESH,
        )

    def when_direct(act):
        def body(turn, step):
            if relay and turn in (1, groups - 1):
                pl.when(group_id != (groups - 1 if turn == 1 else 0))(lambda: act(turn, step))
            else:
                act(turn, step)

        others(body)

    def relay_copy(part, step):
        far = jnp.where(group_id == 1, groups - 1, 0)
        slot = far * tiles + lax.rem(tile_id - step + tiles, tiles)
        end = jnp.where(group_id == 1, 0, groups - 1)
        arrival = jnp.where(group_id == 1, 1, groups - 1) * tiles + step
        return pltpu.make_async_remote_copy(
            src_ref=all_rows.at[slot, :, spans[part]], dst_ref=all_rows.at[slot, :, spans[part]],
            send_sem=relay_send.at[part, step], recv_sem=rows_recv.at[part, arrival],
            device_id={"pulse": end, "tile": tile_id}, device_id_type=MESH,
        )

    last = []
    for part, (start, stop) in enumerate(parts):
        if tiles == TILE_GROUP:
            if part == 0:
                gather(0)
            last = steer(0, start, stop, last)
        else:
            each(tiles // TILE_GROUP, lambda pair: (gather(pair), steer(pair, start, stop, [])))
        when_direct(lambda turn, step: rows_copy(part, turn, step).start())
    keep_own = pltpu.make_async_copy(own_rows.at[tile_id], all_rows.at[me], own_sem)
    keep_own.start()

    others(lambda turn, step: bins_copy(turn, step).wait_recv())
    azimuth_total = AZ_DEV * members
    norm_scale = (pulses * members) ** (-0.5)
    per_member = 2 * pulses
    per_chunk = LANES // per_member
    first_line = tile_id * (groups * AZ_DEV) + group_id * AZ_DEV
    az_line = first_line + lax.broadcasted_iota(jnp.int32, (AZ_DEV, LANES), 0)
    az_lane = lax.broadcasted_iota(jnp.int32, (AZ_DEV, LANES), 1)
    is_imag = (az_lane // pulses) % 2 == 1
    for chunk in range(members // per_chunk):
        known = jnp.zeros((8, LANES), jnp.int32)
        for at in range(per_chunk):
            known = jnp.where(lane // per_member == at, all_bins[chunk * per_chunk + at], known)
        angle = wrap(az_line * known[0:1, :], azimuth_total).astype(jnp.float32) * (2.0 * math.pi / azimuth_total)
        weight = known[1:2, :].astype(jnp.float32) * norm_scale
        factor_re = jnp.cos(angle) * weight
        factor_im = jnp.sin(angle) * weight
        factor_ref[:, chunk * LANES:(chunk + 1) * LANES] = jnp.concatenate(
            [jnp.where(is_imag, -factor_im, factor_re), jnp.where(is_imag, factor_re, factor_im)], axis=0
        ).astype(jnp.bfloat16)

    if relay:
        for part in range(len(parts)):
            others(lambda turn, step: rows_copy(part, turn, step).wait_recv(), [2])

            @pl.when(relays)
            def _():
                each(tiles, lambda step: relay_copy(part, step).start())

    for part in range(len(parts)):
        rest = [turn for turn in turns if not (relay and turn == 2)]
        others(lambda turn, step: rows_copy(part, turn, step).wait_recv(), rest)
    keep_own.wait()

    @pl.when(range_id > 0)
    def _():
        to_left.wait_send()

    @pl.when(range_id < ranges - 1)
    def _():
        to_right.wait_send()

    others(lambda turn, step: bins_copy(turn, step).wait_send())
    for part in range(len(parts)):
        when_direct(lambda turn, step: rows_copy(part, turn, step).wait_send())
    if relay:

        @pl.when(relays)
        def _():
            for part in range(len(parts)):
                each(tiles, lambda step: relay_copy(part, step).wait_send())


def sum_kernel(factor_in, rows_in, out_ref, factor, rows, image, load_sem, store_sem):
    pieces = load_sem.shape[0] - 1
    width = rows.shape[1] // pieces
    load_factor = pltpu.make_async_copy(factor_in, factor, load_sem.at[pieces])
    load_factor.start()
    spans = [pl.ds(piece * width, width) for piece in range(pieces)]
    loads = [
        pltpu.make_async_copy(rows_in.at[:, span], rows.at[:, span], load_sem.at[piece])
        for piece, span in enumerate(spans)
    ]
    stores = [
        pltpu.make_async_copy(image.at[:, span], out_ref.at[:, span], store_sem.at[piece])
        for piece, span in enumerate(spans)
    ]
    for load in loads:
        load.start()
    load_factor.wait()
    for span, load, store in zip(spans, loads, stores):
        load.wait()
        image[:, span] = jnp.dot(factor[...], rows[:, span], preferred_element_type=jnp.float32)
        store.start()
    for store in stores:
        store.wait()


def local(echo, replica, interp, band_start, visible, doppler, range_step):
    chirp_blocks = replica.shape[1] // LANES
    pulses = echo.shape[1]
    samples = echo.shape[2]
    samp_blocks = samples // LANES
    lines = interp.shape[0] * interp.shape[2]
    band_blocks = interp.shape[0] + 1
    tiles = lax.axis_size("tile")
    groups = lax.axis_size("pulse")
    ranges = lax.axis_size("range")
    members = tiles * groups
    half = chirp_blocks * LANES // 2
    rows = TILE_GROUP * pulses
    seen_pad = -(-(band_blocks + chirp_blocks) // 8) * 8
    ext_blocks = samp_blocks + chirp_blocks + 8
    sizes = (pulses, tiles, groups, ranges, band_blocks, chirp_blocks, samp_blocks, lines)
    hbm = pl.BlockSpec(memory_space=pl.ANY)
    vmem = pl.BlockSpec(memory_space=pltpu.VMEM)
    rows_out, factors = pl.pallas_call(
        functools.partial(image_kernel, sizes),
        out_shape=(
            jax.ShapeDtypeStruct((members, 2 * pulses, lines), jnp.bfloat16),
            jax.ShapeDtypeStruct((2 * AZ_DEV, members * 2 * pulses), jnp.bfloat16),
        ),
        in_specs=[hbm] * 7,
        out_specs=(hbm, vmem),
        scratch_shapes=[
            pltpu.SMEM((tiles, 1, pulses), jnp.int32),
            pltpu.SMEM((tiles, pulses), jnp.int32),
            pltpu.SMEM((pulses,), jnp.int32),
            pltpu.SMEM((pulses,), jnp.int32),
            pltpu.VMEM((2 * pulses, samples), jnp.bfloat16),
            pltpu.VMEM(replica.shape, jnp.bfloat16),
            pltpu.VMEM(interp.shape, jnp.bfloat16),
            pltpu.SemaphoreType.DMA((7,)),
            pltpu.VMEM((2 * pulses, half), jnp.bfloat16),
            pltpu.VMEM((2 * pulses, half), jnp.bfloat16),
            pltpu.VMEM((ext_blocks * pulses, LANES), jnp.float32),
            pltpu.VMEM((ext_blocks * pulses, LANES), jnp.float32),
            pltpu.VMEM((seen_pad * rows, LANES), jnp.float32),
            pltpu.VMEM((seen_pad * rows, LANES), jnp.float32),
            pltpu.VMEM((seen_pad * rows, 2 * LANES), jnp.bfloat16),
            pltpu.VMEM((chirp_blocks + 1, 2 * LANES, 2 * LANES), jnp.bfloat16),
            pltpu.VMEM((pulses, lines), jnp.float32),
            pltpu.VMEM((pulses, lines), jnp.float32),
            pltpu.VMEM((tiles, 8, LANES), jnp.int32),
            pltpu.VMEM((members, 8, LANES), jnp.int32),
            pltpu.VMEM((tiles, 2 * pulses, lines), jnp.bfloat16),
            pltpu.SemaphoreType.DMA,
            pltpu.SemaphoreType.DMA((2,)),
            pltpu.SemaphoreType.DMA((2,)),
            pltpu.SemaphoreType.DMA((members,)),
            pltpu.SemaphoreType.DMA((members,)),
            pltpu.SemaphoreType.DMA((2, members)),
            pltpu.SemaphoreType.DMA((2, members)),
            pltpu.SemaphoreType.DMA((2, tiles)),
        ],
        compiler_params=pltpu.CompilerParams(
            collective_id=0, has_side_effects=True, vmem_limit_bytes=60 * 1024 * 1024
        ),
        name="backproject",
    )(
        band_start.transpose(1, 2, 0), visible.T, doppler, range_step,
        echo.reshape(2 * pulses, samples), replica, interp,
    )
    depth = members * 2 * pulses
    pieces = 4
    image = pl.pallas_call(
        sum_kernel,
        out_shape=jax.ShapeDtypeStruct((2 * AZ_DEV, lines), jnp.float32),
        in_specs=[hbm] * 2,
        out_specs=hbm,
        scratch_shapes=[
            pltpu.VMEM((2 * AZ_DEV, depth), jnp.bfloat16),
            pltpu.VMEM((depth, lines), jnp.bfloat16),
            pltpu.VMEM((2 * AZ_DEV, lines), jnp.float32),
            pltpu.SemaphoreType.DMA((pieces + 1,)),
            pltpu.SemaphoreType.DMA((pieces,)),
        ],
        compiler_params=pltpu.CompilerParams(vmem_limit_bytes=60 * 1024 * 1024),
        name="sum_pulses",
    )(factors, rows_out.reshape(depth, lines))
    return image.reshape(2, AZ_DEV, lines)


def solution(mesh):
    in_specs = (
        P(None, ("pulse", "tile"), "range"),
        P(),
        P("range", None, None),
        P(("pulse", "tile"), None, "range"),
        P(("pulse", "tile"), None),
        P(("pulse", "tile")),
        P(("pulse", "tile")),
    )
    out_specs = P(None, ("tile", "pulse"), "range")
    return jax.shard_map(local, mesh=mesh, in_specs=in_specs, out_specs=out_specs, check_vma=False)
```

```python
import functools
import math

import jax
import jax.numpy as jnp
from jax import lax
from jax.experimental import pallas as pl
from jax.experimental.pallas import tpu as pltpu
from jax.sharding import PartitionSpec as P

AZ_DEV = 64
LANES = 128
TILE_GROUP = 2
MESH = pl.DeviceIdType.MESH


def each(count, body, first=0):
    if count <= 16:
        for step in range(first, count):
            body(step)
    else:
        lax.fori_loop(first, count, lambda step, carry: (body(step), carry)[1], 0)


def wrap(value, total):
    if total & (total - 1) == 0:
        return value & (total - 1)
    return lax.rem(value, jnp.int32(total))


def image_kernel(
    sizes,
    starts_in, visible_in, doppler_in, step_in,
    echo_in, replica_in, interp_in,
    all_rows, factor_ref,
    starts_ref, visible_ref, doppler_ref, step_ref,
    echo_ref, replica_ref, interp_ref, load_sem,
    left_halo, right_halo, ext_re, ext_im, gat_re, gat_im, gat, chirp,
    turn_cos, turn_sin, own_bins, all_bins, own_rows, own_sem,
    halo_send, halo_recv, bins_send, bins_recv, rows_send, rows_recv, relay_send,
):
    pulses, tiles, groups, ranges, band_blocks, chirp_blocks, samp_blocks, lines = sizes
    half_blocks = chirp_blocks // 2
    half = half_blocks * LANES
    samples = samp_blocks * LANES
    members = groups * tiles
    seen_blocks = band_blocks + chirp_blocks
    seen_pad = gat_re.shape[0] // (TILE_GROUP * pulses)
    group_id = lax.axis_index("pulse")
    tile_id = lax.axis_index("tile")
    range_id = lax.axis_index("range")
    me = group_id * tiles + tile_id

    turns = [2 % groups] + [turn for turn in range(1, groups) if turn != 2 % groups] + [0]

    def others(body, which=None):
        for turn in turns if which is None else which:
            each(tiles, functools.partial(body, turn), first=1 if turn == 0 else 0)

    def member(turn, step):
        group = lax.rem(group_id + turn, groups)
        tile = lax.rem(tile_id + step, tiles)
        return tile, {"pulse": group, "tile": tile}

    places = (
        (step_in, step_ref), (doppler_in, doppler_ref), (visible_in, visible_ref), (starts_in, starts_ref),
        (replica_in, replica_ref), (echo_in, echo_ref), (interp_in, interp_ref),
    )
    loads = [
        pltpu.make_async_copy(there, here, load_sem.at[place]) for place, (there, here) in enumerate(places)
    ]
    load_step, load_doppler, load_visible, load_starts, load_replica, load_echo, load_interp = loads
    for load in loads:
        load.start()

    barrier = pltpu.get_barrier_semaphore()

    @pl.when(range_id > 0)
    def _():
        pl.semaphore_signal(barrier, inc=1, device_id={"range": range_id - 1}, device_id_type=MESH)

    @pl.when(range_id < ranges - 1)
    def _():
        pl.semaphore_signal(barrier, inc=1, device_id={"range": range_id + 1}, device_id_type=MESH)

    def greet(turn, step):
        _, where = member(turn, step)
        pl.semaphore_signal(barrier, inc=1, device_id=where, device_id_type=MESH)

    others(greet)
    load_step.wait()
    line_number = range_id * lines + lax.broadcasted_iota(jnp.int32, (pulses, lines), 1)
    pulse_row = lax.broadcasted_iota(jnp.int32, (pulses, lines), 0)
    steps = jnp.zeros((pulses, lines), jnp.int32)
    for q in range(pulses):
        steps = jnp.where(pulse_row == q, step_ref[q], steps)
    range_total = lines * ranges
    angle = wrap(steps * line_number, range_total).astype(jnp.float32) * (2.0 * math.pi / range_total)
    turn_cos[...] = jnp.cos(angle)
    turn_sin[...] = jnp.sin(angle)

    neighbours = (range_id > 0).astype(jnp.int32) + (range_id < ranges - 1).astype(jnp.int32)
    pl.semaphore_wait(barrier, members - 1 + neighbours)

    to_left = pltpu.make_async_remote_copy(
        src_ref=echo_in.at[:, pl.ds(0, half)], dst_ref=right_halo,
        send_sem=halo_send.at[0], recv_sem=halo_recv.at[0],
        device_id={"range": lax.max(range_id - 1, 0)}, device_id_type=MESH,
    )
    to_right = pltpu.make_async_remote_copy(
        src_ref=echo_in.at[:, pl.ds(samples - half, half)], dst_ref=left_halo,
        send_sem=halo_send.at[1], recv_sem=halo_recv.at[1],
        device_id={"range": lax.min(range_id + 1, ranges - 1)}, device_id_type=MESH,
    )

    @pl.when(range_id > 0)
    def _():
        to_left.start()

    @pl.when(range_id < ranges - 1)
    def _():
        to_right.start()

    load_doppler.wait()
    load_visible.wait()
    load_starts.wait()
    lane = lax.broadcasted_iota(jnp.int32, (8, LANES), 1)
    row = lax.broadcasted_iota(jnp.int32, (8, LANES), 0)
    lane_pulse = lane % pulses
    bins = jnp.zeros((8, LANES), jnp.int32)
    for q in range(pulses):
        bins = jnp.where(lane_pulse == q, doppler_ref[q], bins)

    def fill_bins(tile):
        flags = jnp.zeros((8, LANES), jnp.int32)
        for q in range(pulses):
            flags = jnp.where(lane_pulse == q, visible_ref[tile, q], flags)
        own_bins[tile] = jnp.where(row == 0, bins, flags)

    each(tiles, fill_bins)

    def bins_copy(turn, step):
        tile, where = member(turn, step)
        return pltpu.make_async_remote_copy(
            src_ref=own_bins.at[tile], dst_ref=all_bins.at[me],
            send_sem=bins_send.at[turn * tiles + step], recv_sem=bins_recv.at[turn * tiles + step],
            device_id=where, device_id_type=MESH,
        )

    others(lambda turn, step: bins_copy(turn, step).start())
    all_bins[me] = own_bins[tile_id]

    load_replica.wait()

    wide = chirp_blocks + 1
    taps = replica_ref[...]
    flip = (
        lax.broadcasted_iota(jnp.int32, (LANES, LANES), 0)
        + lax.broadcasted_iota(jnp.int32, (LANES, LANES), 1) == LANES - 1
    ).astype(jnp.bfloat16)
    by_block = jnp.concatenate([taps[:, block * LANES:(block + 1) * LANES] for block in range(chirp_blocks)], axis=0)
    flipped = jnp.dot(by_block, flip, preferred_element_type=jnp.float32)

    def shifted(part):
        pieces = [flipped[2 * block + part:2 * block + part + 1] for block in reversed(range(chirp_blocks))]
        line = jnp.concatenate([jnp.zeros((1, LANES), jnp.float32)] + pieces, axis=1)
        spread = jnp.broadcast_to(line, (LANES, wide * LANES))
        moved = pltpu.roll(spread, 1, 1, stride=1, stride_axis=0).astype(jnp.bfloat16)
        places = [(wide - turn) % wide for turn in range(wide)]
        return [moved[:, place * LANES:(place + 1) * LANES] for place in places]

    for turn, block in enumerate(shifted(0)):
        chirp[turn, :LANES, :LANES] = block
        chirp[turn, LANES:, LANES:] = block
    for turn, block in enumerate(shifted(1)):
        chirp[turn, LANES:, :LANES] = block
        chirp[turn, :LANES, LANES:] = -block

    def lay(block, values):
        ext_re[block * pulses:(block + 1) * pulses, :] = values[:pulses]
        ext_im[block * pulses:(block + 1) * pulses, :] = values[pulses:]

    load_echo.wait()
    for block in range(samp_blocks):
        lay(half_blocks + block, echo_ref[:, block * LANES:(block + 1) * LANES].astype(jnp.float32))
    filled = samp_blocks + 2 * half_blocks
    tail = ext_re.shape[0] - filled * pulses
    ext_re[filled * pulses:, :] = jnp.zeros((tail, LANES), jnp.float32)
    ext_im[filled * pulses:, :] = jnp.zeros((tail, LANES), jnp.float32)

    @pl.when(range_id > 0)
    def _():
        to_right.wait_recv()

    @pl.when(range_id == 0)
    def _():
        left_halo[...] = jnp.zeros_like(left_halo)

    @pl.when(range_id < ranges - 1)
    def _():
        to_left.wait_recv()

    @pl.when(range_id == ranges - 1)
    def _():
        right_halo[...] = jnp.zeros_like(right_halo)

    for block in range(half_blocks):
        lay(block, left_halo[:, block * LANES:(block + 1) * LANES].astype(jnp.float32))
        lay(
            half_blocks + samp_blocks + block,
            right_halo[:, block * LANES:(block + 1) * LANES].astype(jnp.float32),
        )

    load_interp.wait()

    rows = TILE_GROUP * pulses
    cut = band_blocks // 2 + 1
    parts = [(0, band_blocks)]
    spans = [
        pl.ds(max(start - 1, 0) * LANES, (stop - 1 - max(start - 1, 0)) * LANES) for start, stop in parts
    ]

    def gather(pair):
        for which in range(TILE_GROUP):
            for q in range(pulses):
                first = starts_ref[pair * TILE_GROUP + which, 0, q] // LANES
                source = pl.ds(first * pulses + q, seen_pad, stride=pulses)
                target = pl.ds(which * pulses + q, seen_pad, stride=rows)
                gat_re[target, :] = ext_re[source, :]
                gat_im[target, :] = ext_im[source, :]
        gat[:, :LANES] = gat_re[...].astype(jnp.bfloat16)
        gat[:, LANES:] = gat_im[...].astype(jnp.bfloat16)

    def steer(pair, start, stop, before):
        seen = jnp.concatenate(
            [gat[(turn + start) * rows:(turn + stop) * rows, :] for turn in range(chirp_blocks + 1)], axis=1
        )
        matrix = chirp[...].reshape((chirp_blocks + 1) * 2 * LANES, 2 * LANES)
        total = jnp.dot(seen, matrix, preferred_element_type=jnp.float32)
        made = total.astype(jnp.bfloat16)
        bands = before + [made[j * rows:(j + 1) * rows] for j in range(stop - start)]
        for here, after, j in zip(bands, bands[1:], range(start - len(before), stop - 1)):
            window = jnp.concatenate(
                [
                    jnp.concatenate([here[:, :LANES], after[:, :LANES]], axis=1),
                    jnp.concatenate([here[:, LANES:], after[:, LANES:]], axis=1),
                ],
                axis=0,
            )
            values = jnp.dot(window, interp_ref[j], preferred_element_type=jnp.float32)
            cosine = turn_cos[:, j * LANES:(j + 1) * LANES]
            sine = turn_sin[:, j * LANES:(j + 1) * LANES]
            for which in range(TILE_GROUP):
                real = values[which * pulses:(which + 1) * pulses]
                imag = values[rows + which * pulses:rows + (which + 1) * pulses]
                steered = jnp.concatenate(
                    [real * cosine - imag * sine, real * sine + imag * cosine], axis=0
                )
                own_rows[pair * TILE_GROUP + which, :, j * LANES:(j + 1) * LANES] = steered.astype(jnp.bfloat16)
        return bands[-1:]

    relay = False
    relays = jnp.logical_or(group_id == 1, group_id == groups - 2)

    def rows_copy(part, turn, step):
        tile, where = member(turn, step)
        return pltpu.make_async_remote_copy(
            src_ref=own_rows.at[tile, :, spans[part]], dst_ref=all_rows.at[me, :, spans[part]],
            send_sem=rows_send.at[part, turn * tiles + step], recv_sem=rows_recv.at[part, turn * tiles + step],
            device_id=where, device_id_type=MESH,
        )

    def when_direct(act):
        def body(turn, step):
            if relay and turn in (1, groups - 1):
                pl.when(group_id != (groups - 1 if turn == 1 else 0))(lambda: act(turn, step))
            else:
                act(turn, step)

        others(body)

    def relay_copy(part, step):
        far = jnp.where(group_id == 1, groups - 1, 0)
        slot = far * tiles + lax.rem(tile_id - step + tiles, tiles)
        end = jnp.where(group_id == 1, 0, groups - 1)
        arrival = jnp.where(group_id == 1, 1, groups - 1) * tiles + step
        return pltpu.make_async_remote_copy(
            src_ref=all_rows.at[slot, :, spans[part]], dst_ref=all_rows.at[slot, :, spans[part]],
            send_sem=relay_send.at[part, step], recv_sem=rows_recv.at[part, arrival],
            device_id={"pulse": end, "tile": tile_id}, device_id_type=MESH,
        )

    last = []
    for part, (start, stop) in enumerate(parts):
        if tiles == TILE_GROUP:
            if part == 0:
                gather(0)
            last = steer(0, start, stop, last)
        else:
            each(tiles // TILE_GROUP, lambda pair: (gather(pair), steer(pair, start, stop, [])))
        when_direct(lambda turn, step: rows_copy(part, turn, step).start())
    keep_own = pltpu.make_async_copy(own_rows.at[tile_id], all_rows.at[me], own_sem)
    keep_own.start()

    others(lambda turn, step: bins_copy(turn, step).wait_recv())
    azimuth_total = AZ_DEV * members
    norm_scale = (pulses * members) ** (-0.5)
    per_member = 2 * pulses
    per_chunk = LANES // per_member
    first_line = tile_id * (groups * AZ_DEV) + group_id * AZ_DEV
    az_line = first_line + lax.broadcasted_iota(jnp.int32, (AZ_DEV, LANES), 0)
    az_lane = lax.broadcasted_iota(jnp.int32, (AZ_DEV, LANES), 1)
    is_imag = (az_lane // pulses) % 2 == 1
    for chunk in range(members // per_chunk):
        known = jnp.zeros((8, LANES), jnp.int32)
        for at in range(per_chunk):
            known = jnp.where(lane // per_member == at, all_bins[chunk * per_chunk + at], known)
        angle = wrap(az_line * known[0:1, :], azimuth_total).astype(jnp.float32) * (2.0 * math.pi / azimuth_total)
        weight = known[1:2, :].astype(jnp.float32) * norm_scale
        factor_re = jnp.cos(angle) * weight
        factor_im = jnp.sin(angle) * weight
        factor_ref[:, chunk * LANES:(chunk + 1) * LANES] = jnp.concatenate(
            [jnp.where(is_imag, -factor_im, factor_re), jnp.where(is_imag, factor_re, factor_im)], axis=0
        ).astype(jnp.bfloat16)

    if relay:
        for part in range(len(parts)):
            others(lambda turn, step: rows_copy(part, turn, step).wait_recv(), [2])

            @pl.when(relays)
            def _():
                each(tiles, lambda step: relay_copy(part, step).start())

    for part in range(len(parts)):
        rest = [turn for turn in turns if not (relay and turn == 2)]
        others(lambda turn, step: rows_copy(part, turn, step).wait_recv(), rest)
    keep_own.wait()

    @pl.when(range_id > 0)
    def _():
        to_left.wait_send()

    @pl.when(range_id < ranges - 1)
    def _():
        to_right.wait_send()

    others(lambda turn, step: bins_copy(turn, step).wait_send())
    for part in range(len(parts)):
        when_direct(lambda turn, step: rows_copy(part, turn, step).wait_send())
    if relay:

        @pl.when(relays)
        def _():
            for part in range(len(parts)):
                each(tiles, lambda step: relay_copy(part, step).wait_send())


def local(echo, replica, interp, band_start, visible, doppler, range_step):
    chirp_blocks = replica.shape[1] // LANES
    pulses = echo.shape[1]
    samples = echo.shape[2]
    samp_blocks = samples // LANES
    lines = interp.shape[0] * interp.shape[2]
    band_blocks = interp.shape[0] + 1
    tiles = lax.axis_size("tile")
    groups = lax.axis_size("pulse")
    ranges = lax.axis_size("range")
    members = tiles * groups
    half = chirp_blocks * LANES // 2
    rows = TILE_GROUP * pulses
    seen_pad = -(-(band_blocks + chirp_blocks) // 8) * 8
    ext_blocks = samp_blocks + chirp_blocks + 8
    sizes = (pulses, tiles, groups, ranges, band_blocks, chirp_blocks, samp_blocks, lines)
    hbm = pl.BlockSpec(memory_space=pl.ANY)
    vmem = pl.BlockSpec(memory_space=pltpu.VMEM)
    rows_out, factors = pl.pallas_call(
        functools.partial(image_kernel, sizes),
        out_shape=(
            jax.ShapeDtypeStruct((members, 2 * pulses, lines), jnp.bfloat16),
            jax.ShapeDtypeStruct((2 * AZ_DEV, members * 2 * pulses), jnp.bfloat16),
        ),
        in_specs=[hbm] * 7,
        out_specs=(hbm, vmem),
        scratch_shapes=[
            pltpu.SMEM((tiles, 1, pulses), jnp.int32),
            pltpu.SMEM((tiles, pulses), jnp.int32),
            pltpu.SMEM((pulses,), jnp.int32),
            pltpu.SMEM((pulses,), jnp.int32),
            pltpu.VMEM((2 * pulses, samples), jnp.bfloat16),
            pltpu.VMEM(replica.shape, jnp.bfloat16),
            pltpu.VMEM(interp.shape, jnp.bfloat16),
            pltpu.SemaphoreType.DMA((7,)),
            pltpu.VMEM((2 * pulses, half), jnp.bfloat16),
            pltpu.VMEM((2 * pulses, half), jnp.bfloat16),
            pltpu.VMEM((ext_blocks * pulses, LANES), jnp.float32),
            pltpu.VMEM((ext_blocks * pulses, LANES), jnp.float32),
            pltpu.VMEM((seen_pad * rows, LANES), jnp.float32),
            pltpu.VMEM((seen_pad * rows, LANES), jnp.float32),
            pltpu.VMEM((seen_pad * rows, 2 * LANES), jnp.bfloat16),
            pltpu.VMEM((chirp_blocks + 1, 2 * LANES, 2 * LANES), jnp.bfloat16),
            pltpu.VMEM((pulses, lines), jnp.float32),
            pltpu.VMEM((pulses, lines), jnp.float32),
            pltpu.VMEM((tiles, 8, LANES), jnp.int32),
            pltpu.VMEM((members, 8, LANES), jnp.int32),
            pltpu.VMEM((tiles, 2 * pulses, lines), jnp.bfloat16),
            pltpu.SemaphoreType.DMA,
            pltpu.SemaphoreType.DMA((2,)),
            pltpu.SemaphoreType.DMA((2,)),
            pltpu.SemaphoreType.DMA((members,)),
            pltpu.SemaphoreType.DMA((members,)),
            pltpu.SemaphoreType.DMA((2, members)),
            pltpu.SemaphoreType.DMA((2, members)),
            pltpu.SemaphoreType.DMA((2, tiles)),
        ],
        compiler_params=pltpu.CompilerParams(
            collective_id=0, has_side_effects=True, vmem_limit_bytes=60 * 1024 * 1024
        ),
        name="backproject",
    )(
        band_start.transpose(1, 2, 0), visible.T, doppler, range_step,
        echo.reshape(2 * pulses, samples), replica, interp,
    )
    image = jnp.dot(
        factors, rows_out.reshape(members * 2 * pulses, lines), preferred_element_type=jnp.float32
    )
    return image.reshape(2, AZ_DEV, lines)


def solution(mesh):
    in_specs = (
        P(None, ("pulse", "tile"), "range"),
        P(),
        P("range", None, None),
        P(("pulse", "tile"), None, "range"),
        P(("pulse", "tile"), None),
        P(("pulse", "tile")),
        P(("pulse", "tile")),
    )
    out_specs = P(None, ("tile", "pulse"), "range")
    return jax.shard_map(local, mesh=mesh, in_specs=in_specs, out_specs=out_specs, check_vma=False)
```
